512 devices in a mesh: blk: 64 (over z_lo, y, core), rep: 8 (over x, z_hi).
Axes of the slice: x: 4, y: 4, z: 16 (z_hi: 2, z_lo: 8; z = z_hi * 8 + z_lo), core: 2. Of those that a mesh axis runs over, the one named last changes fastest.
Arguments:
- qm_pos: float32 [3, 8192], P(None, 'blk'), may hold values from -4 to 4
- species: int32 [8192], P('blk'), may hold values from 0 to 7
- qm_count: int32 [64], P('blk'), may hold values from 64 to 128, as said below
- ghost_owner: int32 [8192, 4], P('blk'), may hold values from 0 to 63, all different within a row; in each aligned block of 128 rows (0 to 127, 128 to 255, ...) at most 16 rows name the same one
- ghost_slot: int32 [8192, 4], P('blk'), may hold values from 0 to 127
- mm_pos: float32 [3, 262144], P(None, ('blk', 'rep')), may hold values from -4 to 4
- mm_charge: float32 [262144], P(('blk', 'rep')), may hold values from -6 to 6
- species_table: bfloat16 [8, 128], replicated, may hold values from -6 to 6
- potential_gain: float32 [128], replicated, may hold values from -8 to 8
- message_weight: bfloat16 [128, 128], replicated, may hold values from -0.25 to 0.25
- hidden_weight: bfloat16 [128, 256], replicated, may hold values from -0.5 to 0.5
- energy_readout: float32 [256], replicated, may hold values from -0.375 to 0.375
- charge_readout: float32 [256], replicated, may hold values from -0.375 to 0.375
Outputs:
- atom_energy: float32 [8192], P('blk')
- qm_force: float32 [3, 8192], P(None, 'blk')
- mm_force: float32 [3, 262144], P(None, ('blk', 'rep'))
The draws below stay inside these ranges and needn't reach their ends.
Inputs may be any that keep to these rules, and one draw needn't show every extreme that they name: `qm_count`: some block holds exactly 128 live atoms. `ghost_owner`: each row names 4 different blocks; among the rows of one device no block is named more than 16 times, and some block exactly 16 times.
All inputs are finite; a program needn't handle non-finite values.
Results may differ from the reference program's by a relative error of at most 0.0055.
Values may be sent and summed in bfloat16 or wider, within the bound.
A program may use at most 64 MiB of HBM per device.

```python
import math
import jax
import jax.numpy as jnp
import numpy as np
from jax import lax

A_DEV = 128
F = 128
H = 256
S = 8
K = 4
NQM = 8192
NMM = 262144
CAP = 16
N_BLK = 64


def draw_qm_count(key, part):
    key_counts, key_full = jax.random.split(key)
    counts = jax.random.randint(key_counts, (N_BLK,), A_DEV // 2, A_DEV + 1)
    chosen = jax.random.randint(key_full, (), 0, N_BLK)
    return jnp.where(jnp.arange(N_BLK) == chosen, A_DEV, counts).astype(jnp.int32)


def plant(result, rng, least, high):
    longest = result.shape.index(max(result.shape))
    spots = []
    for shift in (0, 1):
        where = [jax.random.randint(jax.random.fold_in(rng, axis), (), 0, length) for axis, length in enumerate(result.shape)]
        where[longest] = (where[longest] + shift) % result.shape[longest]
        spots.append(tuple(where))
    return result.at[spots[0]].set(least).at[spots[1]].set(high)


def level_of(stream_key, dims, shards, low, high):
    loudness, own = 1.0, jax.random.fold_in(stream_key, 6)
    for position, shards_of in shards:
        draws = jnp.exp(jax.random.uniform(jax.random.fold_in(own, position), (shards_of,), jnp.float32, low / len(shards), high / len(shards)))
        loudness = loudness * jnp.repeat(draws, dims[position] // shards_of).reshape([-1 if axis == position else 1 for axis in range(len(dims))])
    return loudness


def routed_block(stream_key, own, number, rows, number_of, top, limit, lean):
    ranking = jax.random.permutation(stream_key, number_of)
    crowded, common = load_shares(number_of, rows * top, limit, lean, True), load_shares(number_of, rows * top, limit, lean, False)
    places = jnp.arange(number_of)

    def named(sizes, offset_by):
        used = int((sizes > 0).sum())
        fixed = max(1, used // 4)
        passed = fixed + (places - fixed + offset_by * (used - fixed)) % max(1, number_of - fixed)
        return jnp.zeros((number_of,), jnp.int32).at[ranking[jnp.where(places < fixed, places, passed)]].set(jnp.asarray(sizes, jnp.int32))

    sizes = jnp.where(number % 4 == 0, named(crowded, number // 4), named(common, number - number // 4 - 1))
    mixed = jax.random.permutation(jax.random.fold_in(own, 3), number_of)
    giver, receiver = mixed[0:number_of // 2 * 2:2], mixed[1:number_of // 2 * 2:2]
    margin = jnp.minimum(sizes[giver] - 1, limit - sizes[receiver]) // 2
    margin = jnp.where((giver == ranking[0]) | (receiver == ranking[0]) | (sizes[receiver] == 0), 0, jnp.maximum(margin, 0))
    passed = jax.random.randint(jax.random.fold_in(own, 4), (number_of // 2,), 0, 1 << 20) % (margin + 1)
    sizes = sizes.at[giver].add(-passed).at[receiver].add(passed)
    items = jnp.searchsorted(jnp.cumsum(sizes), jnp.arange(rows * top), side="right").astype(jnp.int32)
    listing = items.reshape(top, rows).T
    listing = listing[jax.random.permutation(jax.random.fold_in(own, 1), rows)]
    offset_by = jax.random.randint(jax.random.fold_in(own, 2), (rows, 1), 0, top)
    return jnp.take_along_axis(listing, (jnp.arange(top)[None, :] + offset_by) % top, axis=1)


def load_shares(number_of, total, bound, lean, full):
    portions = [(1 << 20) // math.isqrt(grade ** lean) + 1 for grade in range(1, number_of + 1)]
    largest = bound if full else min(bound, max(-(-total // number_of), total * portions[0] // sum(portions)))
    least = 1 if total - largest >= number_of - 1 else 0
    given, surplus = [largest] + [least] * (number_of - 1), total - largest - least * (number_of - 1)
    while surplus > 0:
        movable = [i for i in range(1, number_of) if given[i] < largest] or [i for i in range(1, number_of) if given[i] < bound]
        pool, remaining = sum([portions[i] for i in movable]), surplus
        for i in movable:
            addition = min(bound - given[i], max(1, remaining * portions[i] // pool), surplus)
            given[i] = given[i] + addition
            surplus = surplus - addition
    return np.array(given)


def noise(rng, extent, scale, reach, pieces=(), kind=jnp.bfloat16):
    result = jax.random.normal(rng, extent, jnp.float32) * scale
    if len(pieces) > 0:
        result = level_of(rng, extent, pieces, -0.22, 0.18) * result
    return jnp.clip(result, min=-reach, max=reach).astype(kind)


def setup_inputs(seed: int = 0) -> dict:
    streams_of = jax.random.split(jax.random.key(seed), 14)
    qm_pos = jnp.clip(jax.random.uniform(streams_of[0], (3, NQM), jnp.float32, -4.0, 4.0) * level_of(streams_of[0], (3, NQM), ((1, 64),), -0.4, 0.0), -4.0, 4.0)
    species = plant(jax.random.randint(streams_of[1], (NQM,), 0, S), jax.random.fold_in(streams_of[1], 1), 0, S - 1).astype(jnp.int32)
    qm_count = draw_qm_count(jax.random.fold_in(streams_of[13], 71), 0)
    ghost_owner_keys = jax.random.split(jax.random.fold_in(streams_of[3], 1), NQM // A_DEV)
    ghost_owner_turns = jax.random.permutation(jax.random.fold_in(streams_of[3], 3), NQM // A_DEV)
    ghost_owner = jax.vmap(lambda own, number: routed_block(jax.random.fold_in(streams_of[3], 2), own, number, A_DEV, N_BLK, K, CAP, 2))(ghost_owner_keys, ghost_owner_turns).reshape((NQM, K))
    ghost_slot = plant(jax.random.randint(streams_of[4], (NQM, K), 0, A_DEV), jax.random.fold_in(streams_of[4], 1), 0, A_DEV - 1).astype(jnp.int32)
    mm_pos = jnp.clip(jax.random.uniform(streams_of[5], (3, NMM), jnp.float32, -4.0, 4.0) * level_of(streams_of[5], (3, NMM), ((1, 512),), -0.4, 0.0), -4.0, 4.0)
    mm_charge = noise(streams_of[6], (NMM,), 1.0, 6.0, ((0, 512),), jnp.float32)
    species_table = noise(streams_of[7], (S, F), 1.0, 6.0)
    potential_gain = noise(streams_of[8], (F,), 2.0, 8.0, (), jnp.float32)
    message_weight = noise(streams_of[9], (F, F), (K * F) ** -0.5, 0.25)
    hidden_weight = noise(streams_of[10], (F, H), F ** -0.5, 0.5)
    energy_readout = noise(streams_of[11], (H,), H ** -0.5, 0.375, (), jnp.float32)
    charge_readout = noise(streams_of[12], (H,), H ** -0.5, 0.375, (), jnp.float32)
    return {"qm_pos": qm_pos, "species": species, "qm_count": qm_count, "ghost_owner": ghost_owner, "ghost_slot": ghost_slot, "mm_pos": mm_pos, "mm_charge": mm_charge, "species_table": species_table, "potential_gain": potential_gain, "message_weight": message_weight, "hidden_weight": hidden_weight, "energy_readout": energy_readout, "charge_readout": charge_readout}


SOFTEN = 0.25

def reference(qm_pos, species, qm_count, ghost_owner, ghost_slot, mm_pos, mm_charge, species_table, potential_gain, message_weight, hidden_weight, energy_readout, charge_readout):
    coupling = float(NMM) ** (-0.5)
    qm_groups = jnp.transpose(qm_pos.reshape(3, N_BLK, A_DEV), (1, 0, 2))

    def potential_block(places):
        offset = places[:, :, None] - mm_pos[:, None, :]
        inverse = lax.rsqrt(lax.optimization_barrier(jnp.sum(offset * offset, axis=0)) + SOFTEN)
        return lax.optimization_barrier(jnp.sum(inverse * mm_charge[None, :], axis=1))
    potential = lax.map(potential_block, qm_groups).reshape(NQM) * coupling
    live = (jnp.arange(A_DEV)[None, :] < qm_count[:, None]).reshape(NQM).astype(jnp.float32)
    picks = (species[:, None] == jnp.arange(S)[None, :]).astype(jnp.bfloat16)
    base = jnp.dot(picks, species_table, preferred_element_type=jnp.float32)
    start = (live[:, None] * (base + potential[:, None] * potential_gain[None, :])).astype(jnp.bfloat16)
    ghost_index = (ghost_owner * A_DEV + ghost_slot).astype(jnp.int32)
    ghosts = jnp.take(start, ghost_index.reshape(-1), axis=0).astype(jnp.float32)
    neighbour = lax.optimization_barrier(jnp.sum(ghosts.reshape(NQM, K, F), axis=1)).astype(jnp.bfloat16)
    mixed = start.astype(jnp.float32) + jnp.dot(neighbour, message_weight, preferred_element_type=jnp.float32)
    mixed_b = mixed.astype(jnp.bfloat16)
    before = jnp.dot(mixed_b, hidden_weight, preferred_element_type=jnp.float32)
    sigma = jax.nn.sigmoid(before)
    active = before * sigma
    energy_part = live * lax.optimization_barrier(jnp.sum(active * energy_readout[None, :], axis=1))
    charge_part = live * lax.optimization_barrier(jnp.sum(active * charge_readout[None, :], axis=1))
    atom_energy = energy_part + charge_part * potential
    back_active = live[:, None] * (energy_readout[None, :] + potential[:, None] * charge_readout[None, :])
    back_before = (back_active * sigma * (1.0 + before * (1.0 - sigma))).astype(jnp.bfloat16)
    back_mixed = jnp.dot(back_before, hidden_weight.T, preferred_element_type=jnp.float32)
    back_sum = jnp.dot(back_mixed.astype(jnp.bfloat16), message_weight.T, preferred_element_type=jnp.float32).astype(jnp.bfloat16)
    spread = jnp.repeat(back_sum.astype(jnp.float32), K, axis=0)
    back_start = back_mixed + jnp.zeros((NQM, F), jnp.float32).at[ghost_index.reshape(-1)].add(spread)
    effective = charge_part + live * lax.optimization_barrier(jnp.sum(back_start * potential_gain[None, :], axis=1))
    stacked = jnp.concatenate([qm_groups, effective.reshape(N_BLK, 1, A_DEV)], axis=1)

    def force_block(mm_running, group):
        offset = group[:3, :, None] - mm_pos[:, None, :]
        inverse = lax.rsqrt(lax.optimization_barrier(jnp.sum(offset * offset, axis=0)) + SOFTEN)
        weight = inverse * inverse * inverse * mm_charge[None, :]
        pull = lax.optimization_barrier(jnp.sum(offset * weight[None], axis=2)) * group[3][None, :]
        mm_running = mm_running - lax.optimization_barrier(jnp.sum(offset * (weight * group[3][:, None])[None], axis=1))
        return (mm_running, pull)
    mm_sum, pulls = lax.scan(force_block, jnp.zeros((3, NMM), jnp.float32), stacked)
    qm_force = jnp.transpose(pulls, (1, 0, 2)).reshape(3, NQM) * coupling
    return (atom_energy, qm_force, mm_sum * coupling)
```

```python
import functools

import jax
import jax.numpy as jnp
from jax import lax
from jax.experimental import pallas as pl
from jax.experimental.pallas import tpu as pltpu
from jax.sharding import PartitionSpec as P

SOFTEN = 0.25
LANES = 128
POT_ROWS = 64
FORCE_ROWS = 32
MESH = pl.DeviceIdType.MESH
F32 = jnp.float32
BF16 = jnp.bfloat16

MM_Z, QM_Q, POT_Q, POT_R, POT_Z, GRAD_Z, GRAD_Q, MMF_Z, QMF_Q, QMF_R = range(10)


def split3(value):
    high = value.astype(BF16)
    rest = value - high.astype(F32)
    middle = rest.astype(BF16)
    low = (rest - middle.astype(F32)).astype(BF16)
    return high, middle, low


def kernel(
    nz,
    nq,
    nr,
    coupling,
    qm_ref,
    species_ref,
    count_ref,
    owner_ref,
    slot_ref,
    mm_ref,
    charge_ref,
    table_ref,
    gain_ref,
    message_ref,
    hidden_ref,
    energy_ref,
    readout_ref,
    atom_energy_ref,
    qm_force_ref,
    mm_force_ref,
    mm_all,
    qm_all,
    pot_q,
    pot_r,
    pot_z,
    grad_mine,
    grad_z,
    grad_sum,
    grad_q,
    mmf_mine,
    mmf_z,
    qmf_mine,
    qmf_q,
    qmf_r,
    wide_x,
    wide_y,
    wide_z,
    wide_e,
    acc_x,
    acc_y,
    acc_z,
    table_wide,
    owner_hot,
    owner_hot_t,
    slot_hot,
    send_sems,
    recv_sems,
):
    blk = lax.axis_index("blk")
    rep = lax.axis_index("rep")
    z = blk // nq
    q = blk % nq
    atoms = qm_ref.shape[1]
    mm_tiles = mm_ref.shape[1] // LANES
    blocks = nz * nq
    neighbours = owner_ref.shape[1]

    along_z = (nz, z, lambda p: (p * nq + q, rep))
    along_q = (nq, q, lambda p: (z * nq + p, rep))
    along_r = (nr, rep, lambda p: (blk, p))

    def copy_to(stage, axis, d, src, dst):
        size, mine, device = axis
        return pltpu.make_async_remote_copy(
            src_ref=src,
            dst_ref=dst,
            send_sem=send_sems.at[stage, d],
            recv_sem=recv_sems.at[stage, d],
            device_id=device((mine + d) % size),
            device_id_type=MESH,
        )

    def each(axis, step):
        def body(d, carry):
            step(d)
            return carry

        lax.fori_loop(1, axis[0], body, 0)

    def send_all(stage, axis, src_of, buffer):
        size, mine, _ = axis

        def step(d):
            copy_to(stage, axis, d, src_of((mine + d) % size), buffer.at[mine]).start()

        each(axis, step)

    def wait_from(stage, axis, d, buffer):
        size, mine, _ = axis
        slot = buffer.at[(mine + size - d) % size]
        copy_to(stage, axis, d, slot, slot).wait_recv()

    def wait_all(stage, axis, buffer):
        each(axis, lambda d: wait_from(stage, axis, d, buffer))

    def sent_all(stage, axis, src_of, buffer):
        size, mine, _ = axis

        def step(d):
            copy_to(stage, axis, d, src_of((mine + d) % size), buffer.at[mine]).wait_send()

        each(axis, step)

    def total(buffer, size):
        result = buffer[0]
        for p in range(1, size):
            result = result + buffer[p]
        return result

    barrier = pltpu.get_barrier_semaphore()
    for axis in (along_z, along_q, along_r):
        size, mine, device = axis

        def greet(d, size=size, mine=mine, device=device):
            pl.semaphore_signal(
                barrier, inc=1, device_id=device((mine + d) % size), device_id_type=MESH
            )

        each(axis, greet)

    mm_all[z, 0:3, :] = mm_ref[...]
    mm_all[z, 3:4, :] = charge_ref[...]
    live_row = lax.broadcasted_iota(jnp.int32, (1, atoms), 1) < count_ref[...]
    qm_all[q, 0:3, :] = qm_ref[...]
    qm_all[q, 3:4, :] = jnp.where(live_row, species_ref[...], -1).astype(F32)

    pl.semaphore_wait(barrier, nz + nq + nr - 3)
    send_all(QM_Q, along_q, lambda p: qm_all.at[q], qm_all)
    send_all(MM_Z, along_z, lambda p: mm_all.at[z], mm_all)

    table_wide[...] = jnp.zeros_like(table_wide)
    table_wide[0 : table_ref.shape[0], :] = table_ref[...].astype(F32)
    lane = lax.broadcasted_iota(jnp.int32, (atoms, LANES), 1)
    row = lax.broadcasted_iota(jnp.int32, (atoms, LANES), 0)
    for k in range(neighbours + 1):
        rows = slice(k * atoms, (k + 1) * atoms)
        if k < neighbours:
            hot = (lane == owner_ref[:, k : k + 1]).astype(F32)
            slots = (lane == slot_ref[:, k : k + 1]).astype(F32)
        else:
            hot = (lane == blk).astype(F32)
            slots = (lane == row).astype(F32)
        owner_hot[rows, :] = hot.astype(BF16)
        owner_hot_t[:, rows] = jnp.transpose(hot)[0 : owner_hot_t.shape[0], :].astype(BF16)
        slot_hot[rows, :] = slots
    acc_x[...] = jnp.zeros_like(acc_x)

    def wide(line):
        return jnp.transpose(jnp.broadcast_to(line, (LANES, atoms)))

    wait_all(QM_Q, along_q, qm_all)

    def widen(p, carry):
        rows = pl.ds(pl.multiple_of(p * atoms, atoms), atoms)
        wide_x[rows, :] = wide(qm_all[p, 0:1, :])
        wide_y[rows, :] = wide(qm_all[p, 1:2, :])
        wide_z[rows, :] = wide(qm_all[p, 2:3, :])
        pot_z[z, pl.ds(nq + p, 1), :] = qm_all[p, 3:4, :]
        return carry

    lax.fori_loop(0, nq, widen, 0)

    def columns(chunk):
        return [
            [mm_all[chunk, c : c + 1, t * LANES : (t + 1) * LANES] for c in range(4)]
            for t in range(mm_tiles)
        ]

    def potential_chunk(d, carry):
        @pl.when(d > 0)
        def _():
            wait_from(MM_Z, along_z, d, mm_all)

        tiles = columns((z + nz - d) % nz)

        def group(g, inner):
            rows = pl.ds(pl.multiple_of(g * POT_ROWS, POT_ROWS), POT_ROWS)
            x, y, w = wide_x[rows, :], wide_y[rows, :], wide_z[rows, :]
            running = acc_x[rows, :]
            for mx, my, mz, mq in tiles:
                dx, dy, dz = x - mx, y - my, w - mz
                inverse = lax.rsqrt(dx * dx + dy * dy + (dz * dz + SOFTEN))
                running = running + inverse * mq
            acc_x[rows, :] = running
            return inner

        return lax.fori_loop(0, nq * atoms // POT_ROWS, group, carry)

    lax.fori_loop(0, nz, potential_chunk, 0)

    def lines(acc, p):
        rows = pl.ds(pl.multiple_of(p * atoms, atoms), atoms)
        return jnp.sum(jnp.transpose(acc[rows, :]), axis=0, keepdims=True)

    def gather_potential(p, carry):
        pot_q[q, pl.ds(p, 1), :] = lines(acc_x, p)
        return carry

    lax.fori_loop(0, nq, gather_potential, 0)
    send_all(POT_Q, along_q, lambda p: pot_q.at[q], pot_q)
    wait_all(POT_Q, along_q, pot_q)
    pot_r[rep] = total(pot_q, nq)
    send_all(POT_R, along_r, lambda p: pot_r.at[rep], pot_r)
    wait_all(POT_R, along_r, pot_r)
    pot_z[z, 0:nq, :] = total(pot_r, nr) * coupling
    send_all(POT_Z, along_z, lambda p: pot_z.at[z], pot_z)
    acc_x[...] = jnp.zeros_like(acc_x)
    acc_y[...] = jnp.zeros_like(acc_y)
    acc_z[...] = jnp.zeros_like(acc_z)
    wait_all(POT_Z, along_z, pot_z)

    potentials = jnp.concatenate([pot_z[p, 0:nq, :] for p in range(nz)], axis=0)
    codes = jnp.concatenate([pot_z[p, nq : 2 * nq, :] for p in range(nz)], axis=0)
    gain = gain_ref[...]
    table = table_wide[...].astype(BF16)
    pieces = [*split3(potentials), codes.astype(BF16)]
    neighbour = jnp.zeros((atoms, LANES), F32)
    for k in range(neighbours + 1):
        rows = slice(k * atoms, (k + 1) * atoms)
        hot = owner_hot[rows, 0:blocks]
        slots = slot_hot[rows, :]
        picked = [jnp.dot(hot, piece, preferred_element_type=F32) for piece in pieces]
        potential = jnp.sum((picked[0] + picked[1] + picked[2]) * slots, axis=1, keepdims=True)
        code = jnp.sum(picked[3] * slots, axis=1, keepdims=True)
        live = (code >= 0).astype(F32)
        kinds = (lane.astype(F32) == code).astype(F32).astype(BF16)
        base = jnp.dot(kinds, table, preferred_element_type=F32)
        start = (live * (base + potential * gain)).astype(BF16)
        if k < neighbours:
            neighbour = neighbour + start.astype(F32)
    mixed = start.astype(F32) + jnp.dot(
        neighbour.astype(BF16), message_ref[...], preferred_element_type=F32
    )
    before = jnp.dot(mixed.astype(BF16), hidden_ref[...], preferred_element_type=F32)
    sigma = jax.nn.sigmoid(before)
    active = before * sigma
    charge_part = live * jnp.sum(active * readout_ref[...], axis=1, keepdims=True)
    back_active = live * (energy_ref[...] + potential * readout_ref[...])
    back_before = (back_active * sigma * (1.0 + before * (1.0 - sigma))).astype(BF16)
    nt = (((1,), (1,)), ((), ()))
    back_mixed = lax.dot_general(back_before, hidden_ref[...], nt, preferred_element_type=F32)
    back_sum = lax.dot_general(
        back_mixed.astype(BF16), message_ref[...], nt, preferred_element_type=F32
    ).astype(BF16)
    out_going = jnp.sum(back_sum.astype(F32) * gain, axis=1, keepdims=True)
    staying = jnp.sum(back_mixed * gain, axis=1, keepdims=True) + charge_part
    spread = jnp.zeros((blocks, LANES), F32)
    parts_out, parts_stay = split3(out_going), split3(staying)
    for k in range(neighbours + 1):
        rows = slice(k * atoms, (k + 1) * atoms)
        slots = slot_hot[rows, :]
        for part in parts_out if k < neighbours else parts_stay:
            spread = spread + jnp.dot(
                owner_hot_t[0:blocks, rows],
                (slots * part.astype(F32)).astype(BF16),
                preferred_element_type=F32,
            )
    for p in range(nz):
        grad_mine[p] = spread[p * nq : (p + 1) * nq, :]
    send_all(GRAD_Z, along_z, lambda p: grad_mine.at[p], grad_z)
    grad_z[z] = grad_mine[z]
    energy_part = live * jnp.sum(active * energy_ref[...], axis=1, keepdims=True)
    atom_energy = energy_part + charge_part * potential
    atom_energy_ref[...] = jnp.sum(
        jnp.where(lane == row, atom_energy, 0.0), axis=0, keepdims=True
    )
    wait_all(GRAD_Z, along_z, grad_z)
    grad_q[q] = total(grad_z, nz)
    send_all(GRAD_Q, along_q, lambda p: grad_q.at[q], grad_q)
    wait_all(GRAD_Q, along_q, grad_q)
    live_plane = (pot_z[z, nq : 2 * nq, :] >= 0).astype(F32)
    grad_sum[...] = live_plane * total(grad_q, nq)

    def widen_effective(p, carry):
        rows = pl.ds(pl.multiple_of(p * atoms, atoms), atoms)
        wide_e[rows, :] = wide(grad_sum[pl.ds(p, 1), :])
        return carry

    lax.fori_loop(0, nq, widen_effective, 0)

    def force_chunk(d, carry):
        chunk = (z + d) % nz
        tiles = columns(chunk)

        def group(g, mm_running):
            rows = pl.ds(pl.multiple_of(g * FORCE_ROWS, FORCE_ROWS), FORCE_ROWS)
            x, y, w, e = wide_x[rows, :], wide_y[rows, :], wide_z[rows, :], wide_e[rows, :]
            fx, fy, fz = acc_x[rows, :], acc_y[rows, :], acc_z[rows, :]
            mm_next = []
            for t, (mx, my, mz, mq) in enumerate(tiles):
                dx, dy, dz = x - mx, y - my, w - mz
                inverse = lax.rsqrt(dx * dx + dy * dy + (dz * dz + SOFTEN))
                cube = inverse * inverse * inverse
                on_qm = cube * mq
                on_mm = cube * e
                fx, fy, fz = fx + on_qm * dx, fy + on_qm * dy, fz + on_qm * dz
                for c, offset in enumerate((dx, dy, dz)):
                    term = jnp.sum((on_mm * offset).reshape(FORCE_ROWS // 8, 8, LANES), axis=0)
                    mm_next.append(mm_running[3 * t + c] + term)
            acc_x[rows, :], acc_y[rows, :], acc_z[rows, :] = fx, fy, fz
            return tuple(mm_next)

        nothing = tuple(jnp.zeros((8, LANES), F32) for _ in range(3 * mm_tiles))
        sums = lax.fori_loop(0, nq * atoms // FORCE_ROWS, group, nothing)
        for t in range(mm_tiles):
            for c in range(3):
                mmf_mine[chunk, c : c + 1, t * LANES : (t + 1) * LANES] = jnp.sum(
                    sums[3 * t + c], axis=0, keepdims=True
                )

        @pl.when(d < nz)
        def _():
            copy_to(MMF_Z, along_z, d, mmf_mine.at[chunk], mmf_z.at[z]).start()

        return carry

    lax.fori_loop(1, nz + 1, force_chunk, 0)
    mmf_z[z] = mmf_mine[z]

    def gather_force(p, carry):
        qmf_mine[p, 0:1, :] = lines(acc_x, p)
        qmf_mine[p, 1:2, :] = lines(acc_y, p)
        qmf_mine[p, 2:3, :] = lines(acc_z, p)
        return carry

    lax.fori_loop(0, nq, gather_force, 0)
    send_all(QMF_Q, along_q, lambda p: qmf_mine.at[p], qmf_q)
    qmf_q[q] = qmf_mine[q]
    wait_all(MMF_Z, along_z, mmf_z)
    mm_force_ref[...] = total(mmf_z, nz) * (charge_ref[...] * -coupling)
    wait_all(QMF_Q, along_q, qmf_q)
    qmf_r[rep] = total(qmf_q, nq)
    send_all(QMF_R, along_r, lambda p: qmf_r.at[rep], qmf_r)
    sent_all(QM_Q, along_q, lambda p: qm_all.at[q], qm_all)
    sent_all(MM_Z, along_z, lambda p: mm_all.at[z], mm_all)
    sent_all(POT_Q, along_q, lambda p: pot_q.at[q], pot_q)
    sent_all(POT_R, along_r, lambda p: pot_r.at[rep], pot_r)
    sent_all(POT_Z, along_z, lambda p: pot_z.at[z], pot_z)
    sent_all(GRAD_Z, along_z, lambda p: grad_mine.at[p], grad_z)
    sent_all(GRAD_Q, along_q, lambda p: grad_q.at[q], grad_q)
    sent_all(MMF_Z, along_z, lambda p: mmf_mine.at[p], mmf_z)
    sent_all(QMF_Q, along_q, lambda p: qmf_mine.at[p], qmf_q)
    wait_all(QMF_R, along_r, qmf_r)
    qm_force_ref[...] = total(qmf_r, nr) * (grad_sum[pl.ds(q, 1), :] * coupling)
    sent_all(QMF_R, along_r, lambda p: qmf_r.at[rep], qmf_r)


def on_device(
    nz,
    nq,
    nr,
    qm_pos,
    species,
    qm_count,
    ghost_owner,
    ghost_slot,
    mm_pos,
    mm_charge,
    species_table,
    potential_gain,
    message_weight,
    hidden_weight,
    energy_readout,
    charge_readout,
):
    atoms = qm_pos.shape[1]
    mm_here = mm_pos.shape[1]
    coupling = float(mm_here * nz * nq * nr) ** (-0.5)
    plane = nq * atoms
    slots = max(nz, nq, nr)
    groups = ghost_owner.shape[1] + 1
    hot_rows = -(-nz * nq // 16) * 16
    small = lambda *shape: pltpu.VMEM(shape, F32)
    vmem = pl.BlockSpec(memory_space=pltpu.VMEM)
    atom_energy, qm_force, mm_force = pl.pallas_call(
        functools.partial(kernel, nz, nq, nr, coupling),
        out_shape=(
            jax.ShapeDtypeStruct((1, atoms), F32),
            jax.ShapeDtypeStruct((3, atoms), F32),
            jax.ShapeDtypeStruct((3, mm_here), F32),
        ),
        in_specs=[vmem] * 13,
        out_specs=(vmem,) * 3,
        scratch_shapes=[
            small(nz, 4, mm_here),
            small(nq, 4, atoms),
            small(nq, nq, atoms),
            small(nr, nq, atoms),
            small(nz, 2 * nq, atoms),
            small(nz, nq, atoms),
            small(nz, nq, atoms),
            small(nq, atoms),
            small(nq, nq, atoms),
            small(nz, 3, mm_here),
            small(nz, 3, mm_here),
            small(nq, 3, atoms),
            small(nq, 3, atoms),
            small(nr, 3, atoms),
            small(plane, LANES),
            small(plane, LANES),
            small(plane, LANES),
            small(plane, LANES),
            small(plane, LANES),
            small(plane, LANES),
            small(plane, LANES),
            small(LANES, LANES),
            pltpu.VMEM((groups * atoms, LANES), BF16),
            pltpu.VMEM((hot_rows, groups * atoms), BF16),
            small(groups * atoms, LANES),
            pltpu.SemaphoreType.DMA((10, slots)),
            pltpu.SemaphoreType.DMA((10, slots)),
        ],
        compiler_params=pltpu.CompilerParams(
            collective_id=0, has_side_effects=True, vmem_limit_bytes=40 * 2**20
        ),
    )(
        qm_pos,
        species[None, :],
        qm_count[None, :],
        ghost_owner,
        ghost_slot,
        mm_pos,
        mm_charge[None, :],
        species_table,
        potential_gain[None, :],
        message_weight,
        hidden_weight,
        energy_readout[None, :],
        charge_readout[None, :],
    )
    return (atom_energy[0], qm_force, mm_force)


def solution(mesh):
    blocks, nr = mesh.shape["blk"], mesh.shape["rep"]
    nq = min(8, blocks // 2)
    placed = (
        P(None, "blk"),
        P("blk"),
        P("blk"),
        P("blk", None),
        P("blk", None),
        P(None, ("blk", "rep")),
        P(("blk", "rep")),
        P(),
        P(),
        P(),
        P(),
        P(),
        P(),
    )
    return jax.shard_map(
        functools.partial(on_device, blocks // nq, nq, nr),
        mesh=mesh,
        in_specs=placed,
        out_specs=(P("blk"), P(None, "blk"), P(None, ("blk", "rep"))),
        check_vma=False,
    )
```

```python
import functools

import jax
import jax.numpy as jnp
from jax import lax
from jax.experimental import pallas as pl
from jax.experimental.pallas import tpu as pltpu
from jax.sharding import PartitionSpec as P

SOFTEN = 0.25
LANES = 128
POT_ROWS = 64
FORCE_ROWS = 32
EARLY = 2
MESH = pl.DeviceIdType.MESH
F32 = jnp.float32
BF16 = jnp.bfloat16

QM_N, MM_Q, POT_X, POT_Z, POT_Q, GRAD_Q, GRAD_N, QMF_Z, QMF_X, MMF_Q = range(10)


def split3(value):
    high = value.astype(BF16)
    rest = value - high.astype(F32)
    middle = rest.astype(BF16)
    low = (rest - middle.astype(F32)).astype(BF16)
    return high, middle, low


def kernel(
    nz,
    nq,
    nx,
    coupling,
    qm_ref,
    species_ref,
    count_ref,
    owner_ref,
    slot_ref,
    mm_ref,
    charge_ref,
    table_ref,
    gain_ref,
    message_ref,
    hidden_ref,
    energy_ref,
    readout_ref,
    atom_energy_ref,
    qm_force_ref,
    mm_force_ref,
    mm_all,
    qm_all,
    pot_x,
    pot_z,
    pot_q,
    grad_mine,
    grad_q,
    grad_n,
    grad_sum,
    qmf_mine,
    qmf_z,
    qmf_x,
    mmf_mine,
    mmf_q,
    wide_x,
    wide_y,
    wide_z,
    wide_e,
    wide_ex,
    wide_ey,
    wide_ez,
    acc_x,
    acc_y,
    acc_z,
    inverses,
    table_wide,
    owner_hot,
    owner_hot_t,
    slot_hot,
    send_sems,
    recv_sems,
):
    blk = lax.axis_index("blk")
    rep = lax.axis_index("rep")
    z, q = blk // nq, blk % nq
    x, ring = rep // 2, (rep % 2) * nz + z
    rings = 2 * nz
    atoms = qm_ref.shape[1]
    mm_tiles = mm_ref.shape[1] // LANES
    blocks = nz * nq
    neighbours = owner_ref.shape[1]

    def at_ring(p):
        return ((p % nz) * nq + q, x * 2 + p // nz)

    def at_q(p):
        return (z * nq + p, rep)

    def shift(d):
        return jnp.where(d < nz // 2, d, d - nz)

    def q_place(d, sign):
        y = (q // 2 + (nq // 2) + sign * (d // 2)) % (nq // 2)
        return y * 2 + (q + d) % 2

    same = lambda p: p
    near = (nz, ring, lambda d: (ring + rings - shift(d)) % rings, lambda d: (ring + rings + shift(d)) % rings, at_ring, lambda p: p % nz)
    far = (rings, ring, lambda d: (ring + d) % rings, lambda d: (ring + rings - d) % rings, at_ring, same)
    plane = (nq, q, lambda d: q_place(d, 1), lambda d: q_place(d, -1), at_q, same)
    row_x = (nx, x, lambda d: (x + d) % nx, lambda d: (x + nx - d) % nx, lambda p: (blk, p * 2 + rep % 2), same)

    def copy_to(stage, d, device, src, dst):
        return pltpu.make_async_remote_copy(
            src_ref=src,
            dst_ref=dst,
            send_sem=send_sems.at[stage, d],
            recv_sem=recv_sems.at[stage, d],
            device_id=device,
            device_id_type=MESH,
        )

    def each(axis, step):
        def body(d, carry):
            step(d)
            return carry

        lax.fori_loop(1, axis[0], body, 0)

    def outgoing(stage, axis, src_of, buffer, d):
        _, mine, to, _, device, slot = axis
        p = to(d)
        return copy_to(stage, d, device(p), src_of(p), buffer.at[slot(mine)])

    def send_all(stage, axis, src_of, buffer):
        each(axis, lambda d: outgoing(stage, axis, src_of, buffer, d).start())

    def sent_all(stage, axis, src_of, buffer):
        each(axis, lambda d: outgoing(stage, axis, src_of, buffer, d).wait_send())

    def wait_from(stage, axis, d, buffer):
        _, _, _, came, device, slot = axis
        p = came(d)
        place = buffer.at[slot(p)]
        copy_to(stage, d, device(p), place, place).wait_recv()
        return slot(p)

    def wait_all(stage, axis, buffer):
        def step(d):
            wait_from(stage, axis, d, buffer)

        each(axis, step)

    def total(buffer, size):
        result = buffer[0]
        for p in range(1, size):
            result = result + buffer[p]
        return result

    barrier = pltpu.get_barrier_semaphore()
    for axis in (far, plane, row_x):

        def greet(d, axis=axis):
            pl.semaphore_signal(barrier, inc=1, device_id=axis[4](axis[2](d)), device_id_type=MESH)

        each(axis, greet)

    mm_all[q, 0:3, :] = mm_ref[...]
    mm_all[q, 3:4, :] = charge_ref[...]
    live_row = lax.broadcasted_iota(jnp.int32, (1, atoms), 1) < count_ref[...]
    qm_all[z, 0:3, :] = qm_ref[...]
    qm_all[z, 3:4, :] = jnp.where(live_row, species_ref[...], -1).astype(F32)

    pl.semaphore_wait(barrier, rings + nq + nx - 3)
    send_all(QM_N, near, lambda p: qm_all.at[z], qm_all)
    send_all(MM_Q, plane, lambda p: mm_all.at[q], mm_all)

    table_wide[...] = jnp.zeros_like(table_wide)
    table_wide[0 : table_ref.shape[0], :] = table_ref[...].astype(F32)
    lane = lax.broadcasted_iota(jnp.int32, (atoms, LANES), 1)
    row = lax.broadcasted_iota(jnp.int32, (atoms, LANES), 0)
    for k in range(neighbours + 1):
        rows = slice(k * atoms, (k + 1) * atoms)
        if k < neighbours:
            owner = owner_ref[:, k : k + 1]
            hot = (lane == (owner % nq) * nz + owner // nq).astype(F32)
            slots = (lane == slot_ref[:, k : k + 1]).astype(F32)
        else:
            hot = (lane == q * nz + z).astype(F32)
            slots = (lane == row).astype(F32)
        owner_hot[rows, :] = hot.astype(BF16)
        owner_hot_t[:, rows] = jnp.transpose(hot)[0 : owner_hot_t.shape[0], :].astype(BF16)
        slot_hot[rows, :] = slots
    acc_x[...] = jnp.zeros_like(acc_x)

    def wide(line):
        return jnp.transpose(jnp.broadcast_to(line, (LANES, atoms)))

    def block_rows(p):
        return pl.ds(pl.multiple_of(p * atoms, atoms), atoms)

    def widen(p):
        rows = block_rows(p)
        wide_x[rows, :] = wide(qm_all[p, 0:1, :])
        wide_y[rows, :] = wide(qm_all[p, 1:2, :])
        wide_z[rows, :] = wide(qm_all[p, 2:3, :])
        pot_q[q, pl.ds(nz + p, 1), :] = qm_all[p, 3:4, :]

    widen(z)
    each(near, lambda d: widen(wait_from(QM_N, near, d, qm_all)))

    def columns(chunk):
        return [
            [mm_all[chunk, c : c + 1, t * LANES : (t + 1) * LANES] for c in range(4)]
            for t in range(mm_tiles)
        ]

    def potential_chunk(d, carry):
        @pl.when(d > 0)
        def _():
            wait_from(MM_Q, plane, d, mm_all)

        chunk = plane[3](d)
        tiles = columns(chunk)

        def group(g, inner):
            rows = pl.ds(pl.multiple_of(g * POT_ROWS, POT_ROWS), POT_ROWS)
            px, py, pz = wide_x[rows, :], wide_y[rows, :], wide_z[rows, :]
            running = acc_x[rows, :]
            for t, (mx, my, mz, mq) in enumerate(tiles):
                dx, dy, dz = px - mx, py - my, pz - mz
                inverse = lax.rsqrt(dx * dx + dy * dy + (dz * dz + SOFTEN))
                inverses[chunk, rows, t * LANES : (t + 1) * LANES] = inverse
                running = running + inverse * mq
            acc_x[rows, :] = running
            return inner

        return lax.fori_loop(0, nz * atoms // POT_ROWS, group, carry)

    lax.fori_loop(0, nq, potential_chunk, 0)

    def lines(acc, p):
        return jnp.sum(jnp.transpose(acc[block_rows(p), :]), axis=0, keepdims=True)

    def gather_potential(p, carry):
        pot_x[x, pl.ds(p, 1), :] = lines(acc_x, p)
        return carry

    lax.fori_loop(0, nz, gather_potential, 0)
    send_all(POT_X, row_x, lambda p: pot_x.at[x], pot_x)
    acc_x[...] = jnp.zeros_like(acc_x)
    acc_y[...] = jnp.zeros_like(acc_y)
    acc_z[...] = jnp.zeros_like(acc_z)

    def pull_chunk(chunk, carry):
        tiles = columns(chunk)

        def group(g, inner):
            rows = pl.ds(pl.multiple_of(g * FORCE_ROWS, FORCE_ROWS), FORCE_ROWS)
            px, py, pz = wide_x[rows, :], wide_y[rows, :], wide_z[rows, :]
            fx, fy, fz = acc_x[rows, :], acc_y[rows, :], acc_z[rows, :]
            for t, (mx, my, mz, mq) in enumerate(tiles):
                where = slice(t * LANES, (t + 1) * LANES)
                inverse = inverses[chunk, rows, where]
                cube = inverse * inverse * inverse
                inverses[chunk, rows, where] = cube
                pull = cube * mq
                fx = fx + pull * (px - mx)
                fy = fy + pull * (py - my)
                fz = fz + pull * (pz - mz)
            acc_x[rows, :], acc_y[rows, :], acc_z[rows, :] = fx, fy, fz
            return inner

        return lax.fori_loop(0, nz * atoms // FORCE_ROWS, group, carry)

    early = min(EARLY, nq)
    lax.fori_loop(0, early, pull_chunk, 0)
    wait_all(POT_X, row_x, pot_x)
    pot_z[ring] = total(pot_x, nx)
    send_all(POT_Z, far, lambda p: pot_z.at[ring], pot_z)
    lax.fori_loop(early, nq, pull_chunk, 0)

    def gather_force(p, carry):
        qmf_mine[p, 0:1, :] = lines(acc_x, p)
        qmf_mine[p, 1:2, :] = lines(acc_y, p)
        qmf_mine[p, 2:3, :] = lines(acc_z, p)
        return carry

    lax.fori_loop(0, nz, gather_force, 0)
    qmf_z[ring] = qmf_mine[z]
    wait_all(POT_Z, far, pot_z)
    pot_q[q, 0:nz, :] = total(pot_z, rings) * coupling
    send_all(POT_Q, plane, lambda p: pot_q.at[q], pot_q)
    send_all(QMF_Z, far, lambda p: qmf_mine.at[p % nz], qmf_z)
    wait_all(POT_Q, plane, pot_q)

    potentials = jnp.concatenate([pot_q[p, 0:nz, :] for p in range(nq)], axis=0)
    codes = jnp.concatenate([pot_q[p, nz : 2 * nz, :] for p in range(nq)], axis=0)
    gain = gain_ref[...]
    table = table_wide[...].astype(BF16)
    pieces = [*split3(potentials), codes.astype(BF16)]
    neighbour = jnp.zeros((atoms, LANES), F32)
    for k in range(neighbours + 1):
        rows = slice(k * atoms, (k + 1) * atoms)
        hot = owner_hot[rows, 0:blocks]
        slots = slot_hot[rows, :]
        picked = [jnp.dot(hot, piece, preferred_element_type=F32) for piece in pieces]
        potential = jnp.sum((picked[0] + picked[1] + picked[2]) * slots, axis=1, keepdims=True)
        code = jnp.sum(picked[3] * slots, axis=1, keepdims=True)
        live = (code >= 0).astype(F32)
        kinds = (lane.astype(F32) == code).astype(F32).astype(BF16)
        base = jnp.dot(kinds, table, preferred_element_type=F32)
        start = (live * (base + potential * gain)).astype(BF16)
        if k < neighbours:
            neighbour = neighbour + start.astype(F32)
    mixed = start.astype(F32) + jnp.dot(
        neighbour.astype(BF16), message_ref[...], preferred_element_type=F32
    )
    before = jnp.dot(mixed.astype(BF16), hidden_ref[...], preferred_element_type=F32)
    sigma = jax.nn.sigmoid(before)
    active = before * sigma
    charge_part = live * jnp.sum(active * readout_ref[...], axis=1, keepdims=True)
    back_active = live * (energy_ref[...] + potential * readout_ref[...])
    back_before = (back_active * sigma * (1.0 + before * (1.0 - sigma))).astype(BF16)
    nt = (((1,), (1,)), ((), ()))
    back_mixed = lax.dot_general(back_before, hidden_ref[...], nt, preferred_element_type=F32)
    back_sum = lax.dot_general(
        back_mixed.astype(BF16), message_ref[...], nt, preferred_element_type=F32
    ).astype(BF16)
    out_going = jnp.sum(back_sum.astype(F32) * gain, axis=1, keepdims=True)
    staying = jnp.sum(back_mixed * gain, axis=1, keepdims=True) + charge_part
    spread = jnp.zeros((blocks, LANES), F32)
    parts_out, parts_stay = split3(out_going), split3(staying)
    for k in range(neighbours + 1):
        rows = slice(k * atoms, (k + 1) * atoms)
        slots = slot_hot[rows, :]
        for part in parts_out if k < neighbours else parts_stay:
            spread = spread + jnp.dot(
                owner_hot_t[0:blocks, rows],
                (slots * part.astype(F32)).astype(BF16),
                preferred_element_type=F32,
            )
    for p in range(nq):
        grad_mine[p] = spread[p * nz : (p + 1) * nz, :]
    send_all(GRAD_Q, plane, lambda p: grad_mine.at[p], grad_q)
    grad_q[q] = grad_mine[q]
    energy_part = live * jnp.sum(active * energy_ref[...], axis=1, keepdims=True)
    atom_energy = energy_part + charge_part * potential
    atom_energy_ref[...] = jnp.sum(
        jnp.where(lane == row, atom_energy, 0.0), axis=0, keepdims=True
    )
    wait_all(GRAD_Q, plane, grad_q)
    grad_n[z] = total(grad_q, nq)
    send_all(GRAD_N, near, lambda p: grad_n.at[z], grad_n)
    wait_all(QMF_Z, far, qmf_z)
    qmf_x[x] = total(qmf_z, rings)
    send_all(QMF_X, row_x, lambda p: qmf_x.at[x], qmf_x)
    wait_all(GRAD_N, near, grad_n)
    live_plane = (pot_q[q, nz : 2 * nz, :] >= 0).astype(F32)
    grad_sum[...] = live_plane * total(grad_n, nz)

    def widen_effective(p, carry):
        rows = block_rows(p)
        effective = wide(grad_sum[pl.ds(p, 1), :])
        wide_e[rows, :] = effective
        wide_ex[rows, :] = effective * wide_x[rows, :]
        wide_ey[rows, :] = effective * wide_y[rows, :]
        wide_ez[rows, :] = effective * wide_z[rows, :]
        return carry

    lax.fori_loop(0, nz, widen_effective, 0)

    def push_chunk(step, carry):
        d = nq - step
        chunk = jnp.where(d > 0, plane[2](d), q)

        def group(g, running):
            rows = pl.ds(pl.multiple_of(g * FORCE_ROWS, FORCE_ROWS), FORCE_ROWS)
            weights = wide_e[rows, :], wide_ex[rows, :], wide_ey[rows, :], wide_ez[rows, :]
            after = []
            for t in range(mm_tiles):
                cube = inverses[chunk, rows, t * LANES : (t + 1) * LANES]
                for c, weight in enumerate(weights):
                    term = jnp.sum((cube * weight).reshape(FORCE_ROWS // 8, 8, LANES), axis=0)
                    after.append(running[4 * t + c] + term)
            return tuple(after)

        nothing = tuple(jnp.zeros((8, LANES), F32) for _ in range(4 * mm_tiles))
        sums = lax.fori_loop(0, nz * atoms // FORCE_ROWS, group, nothing)
        for t in range(mm_tiles):
            where = slice(t * LANES, (t + 1) * LANES)
            plain, *moments = [jnp.sum(sums[4 * t + c], axis=0, keepdims=True) for c in range(4)]
            for c in range(3):
                mmf_mine[chunk, c : c + 1, where] = moments[c] - plain * mm_all[chunk, c : c + 1, where]

        @pl.when(d > 0)
        def _():
            outgoing(MMF_Q, plane, lambda p: mmf_mine.at[p], mmf_q, d).start()

        return carry

    lax.fori_loop(1, nq + 1, push_chunk, 0)
    mmf_q[q] = mmf_mine[q]
    sent_all(QM_N, near, lambda p: qm_all.at[z], qm_all)
    sent_all(MM_Q, plane, lambda p: mm_all.at[q], mm_all)
    sent_all(POT_X, row_x, lambda p: pot_x.at[x], pot_x)
    sent_all(POT_Z, far, lambda p: pot_z.at[ring], pot_z)
    sent_all(POT_Q, plane, lambda p: pot_q.at[q], pot_q)
    sent_all(QMF_Z, far, lambda p: qmf_mine.at[p % nz], qmf_z)
    sent_all(GRAD_Q, plane, lambda p: grad_mine.at[p], grad_q)
    sent_all(GRAD_N, near, lambda p: grad_n.at[z], grad_n)
    wait_all(QMF_X, row_x, qmf_x)
    qm_force_ref[...] = total(qmf_x, nx) * (grad_sum[pl.ds(z, 1), :] * coupling)
    sent_all(QMF_X, row_x, lambda p: qmf_x.at[x], qmf_x)
    sent_all(MMF_Q, plane, lambda p: mmf_mine.at[p], mmf_q)
    wait_all(MMF_Q, plane, mmf_q)
    mm_force_ref[...] = total(mmf_q, nq) * (charge_ref[...] * -coupling)


def on_device(
    nz,
    nq,
    nr,
    qm_pos,
    species,
    qm_count,
    ghost_owner,
    ghost_slot,
    mm_pos,
    mm_charge,
    species_table,
    potential_gain,
    message_weight,
    hidden_weight,
    energy_readout,
    charge_readout,
):
    atoms = qm_pos.shape[1]
    mm_here = mm_pos.shape[1]
    nx = nr // 2
    coupling = float(mm_here * nz * nq * nr) ** (-0.5)
    here = nz * atoms
    groups = ghost_owner.shape[1] + 1
    hot_rows = -(-nz * nq // 16) * 16
    small = lambda *shape: pltpu.VMEM(shape, F32)
    vmem = pl.BlockSpec(memory_space=pltpu.VMEM)
    atom_energy, qm_force, mm_force = pl.pallas_call(
        functools.partial(kernel, nz, nq, nx, coupling),
        out_shape=(
            jax.ShapeDtypeStruct((1, atoms), F32),
            jax.ShapeDtypeStruct((3, atoms), F32),
            jax.ShapeDtypeStruct((3, mm_here), F32),
        ),
        in_specs=[vmem] * 13,
        out_specs=(vmem,) * 3,
        scratch_shapes=[
            small(nq, 4, mm_here),
            small(nz, 4, atoms),
            small(nx, nz, atoms),
            small(2 * nz, nz, atoms),
            small(nq, 2 * nz, atoms),
            small(nq, nz, atoms),
            small(nq, nz, atoms),
            small(nz, nz, atoms),
            small(nz, atoms),
            small(nz, 3, atoms),
            small(2 * nz, 3, atoms),
            small(nx, 3, atoms),
            small(nq, 3, mm_here),
            small(nq, 3, mm_here),
            *[small(here, LANES)] * 10,
            small(nq, here, mm_here),
            small(LANES, LANES),
            pltpu.VMEM((groups * atoms, LANES), BF16),
            pltpu.VMEM((hot_rows, groups * atoms), BF16),
            small(groups * atoms, LANES),
            pltpu.SemaphoreType.DMA((10, max(2 * nz, nq, nx))),
            pltpu.SemaphoreType.DMA((10, max(2 * nz, nq, nx))),
        ],
        compiler_params=pltpu.CompilerParams(
            collective_id=0, has_side_effects=True, vmem_limit_bytes=48 * 2**20
        ),
    )(
        qm_pos,
        species[None, :],
        qm_count[None, :],
        ghost_owner,
        ghost_slot,
        mm_pos,
        mm_charge[None, :],
        species_table,
        potential_gain[None, :],
        message_weight,
        hidden_weight,
        energy_readout[None, :],
        charge_readout[None, :],
    )
    return (atom_energy[0], qm_force, mm_force)


def solution(mesh):
    blocks, nr = mesh.shape["blk"], mesh.shape["rep"]
    nq = min(8, blocks // 2)
    placed = (
        P(None, "blk"),
        P("blk"),
        P("blk"),
        P("blk", None),
        P("blk", None),
        P(None, ("blk", "rep")),
        P(("blk", "rep")),
        P(),
        P(),
        P(),
        P(),
        P(),
        P(),
    )
    return jax.shard_map(
        functools.partial(on_device, blocks // nq, nq, nr),
        mesh=mesh,
        in_specs=placed,
        out_specs=(P("blk"), P(None, "blk"), P(None, ("blk", "rep"))),
        check_vma=False,
    )
```

```python
import functools

import jax
import jax.numpy as jnp
from jax import lax
from jax.experimental import pallas as pl
from jax.experimental.pallas import tpu as pltpu
from jax.sharding import PartitionSpec as P

SOFTEN = 0.25
LANES = 128
FORCE_ROWS = 32
EARLY = 2
MESH = pl.DeviceIdType.MESH
F32 = jnp.float32
BF16 = jnp.bfloat16

QM_N, MM_Q, POT_X, POT_Z, POT_Q, GRAD_Q, GRAD_N, QMF_Z, QMF_X, MMF_Q = range(10)


def split3(value):
    high = value.astype(BF16)
    rest = value - high.astype(F32)
    middle = rest.astype(BF16)
    low = (rest - middle.astype(F32)).astype(BF16)
    return high, middle, low


def kernel(
    nz,
    nq,
    nx,
    coupling,
    qm_ref,
    species_ref,
    count_ref,
    owner_ref,
    slot_ref,
    mm_ref,
    charge_ref,
    table_ref,
    gain_ref,
    message_ref,
    hidden_ref,
    energy_ref,
    readout_ref,
    atom_energy_ref,
    qm_force_ref,
    mm_force_ref,
    mm_all,
    qm_all,
    pot_x,
    pot_z,
    pot_q,
    grad_mine,
    grad_q,
    grad_n,
    grad_sum,
    qmf_mine,
    qmf_z,
    qmf_x,
    mmf_mine,
    mmf_q,
    wide_x,
    wide_y,
    wide_z,
    acc_x,
    acc_y,
    acc_z,
    inverses,
    qm_parts,
    mm_parts,
    charges,
    qm_lines,
    table_wide,
    owner_hot,
    owner_hot_t,
    slot_hot,
    send_sems,
    recv_sems,
):
    blk = lax.axis_index("blk")
    rep = lax.axis_index("rep")
    z, q = blk // nq, blk % nq
    x, ring = rep // 2, (rep % 2) * nz + z
    rings = 2 * nz
    atoms = qm_ref.shape[1]
    mm_tiles = mm_ref.shape[1] // LANES
    blocks = nz * nq
    neighbours = owner_ref.shape[0]

    def at_ring(p):
        return ((p % nz) * nq + q, x * 2 + p // nz)

    def at_q(p):
        return (z * nq + p, rep)

    def shift(d):
        return (d + 1) // 2 * (2 * (d % 2) - 1)

    def q_place(d, sign):
        y = (q // 2 + (nq // 2) + sign * (d // 2)) % (nq // 2)
        return y * 2 + (q + d) % 2

    same = lambda p: p
    near = (nz, ring, lambda d: (ring + rings - shift(d)) % rings, lambda d: (ring + rings + shift(d)) % rings, at_ring, lambda p: p % nz)
    far = (rings, ring, lambda d: (ring + d) % rings, lambda d: (ring + rings - d) % rings, at_ring, same)
    plane = (nq, q, lambda d: q_place(d, 1), lambda d: q_place(d, -1), at_q, same)
    row_x = (nx, x, lambda d: (x + d) % nx, lambda d: (x + nx - d) % nx, lambda p: (blk, p * 2 + rep % 2), same)

    def copy_to(stage, d, device, src, dst):
        return pltpu.make_async_remote_copy(
            src_ref=src,
            dst_ref=dst,
            send_sem=send_sems.at[stage, d],
            recv_sem=recv_sems.at[stage, d],
            device_id=device,
            device_id_type=MESH,
        )

    def each(axis, step):
        def body(d, carry):
            step(d)
            return carry

        lax.fori_loop(1, axis[0], body, 0)

    def outgoing(stage, axis, src_of, buffer, d):
        _, mine, to, _, device, slot = axis
        p = to(d)
        return copy_to(stage, d, device(p), src_of(p), buffer.at[slot(mine)])

    def send_all(stage, axis, src_of, buffer):
        each(axis, lambda d: outgoing(stage, axis, src_of, buffer, d).start())

    def sent_all(stage, axis, src_of, buffer):
        each(axis, lambda d: outgoing(stage, axis, src_of, buffer, d).wait_send())

    def wait_from(stage, axis, d, buffer):
        _, _, _, came, device, slot = axis
        p = came(d)
        place = buffer.at[slot(p)]
        copy_to(stage, d, device(p), place, place).wait_recv()
        return slot(p)

    def wait_all(stage, axis, buffer):
        def step(d):
            wait_from(stage, axis, d, buffer)

        each(axis, step)

    def total(buffer, size):
        result = buffer[0]
        for p in range(1, size):
            result = result + buffer[p]
        return result

    barrier = pltpu.get_barrier_semaphore()
    for axis in (far, plane, row_x):

        def greet(d, axis=axis):
            pl.semaphore_signal(barrier, inc=1, device_id=axis[4](axis[2](d)), device_id_type=MESH)

        each(axis, greet)

    mm_all[q, 0:3, :] = mm_ref[...]
    mm_all[q, 3:4, :] = charge_ref[...]
    live_row = lax.broadcasted_iota(jnp.int32, (1, atoms), 1) < count_ref[...]
    qm_all[z, 0:3, :] = qm_ref[...]
    qm_all[z, 3:4, :] = jnp.where(live_row, species_ref[...], -1).astype(F32)

    pl.semaphore_wait(barrier, rings + nq + nx - 3)
    send_all(QM_N, near, lambda p: qm_all.at[z], qm_all)
    send_all(MM_Q, plane, lambda p: mm_all.at[q], mm_all)

    table_wide[...] = jnp.zeros_like(table_wide)
    table_wide[0 : table_ref.shape[0], :] = table_ref[...].astype(F32)
    lane = lax.broadcasted_iota(jnp.int32, (atoms, LANES), 1)
    row = lax.broadcasted_iota(jnp.int32, (atoms, LANES), 0)
    for k in range(neighbours + 1):
        rows = slice(k * atoms, (k + 1) * atoms)
        if k < neighbours:
            owner = owner_ref[k : k + 1, :]
            hot_t = (row == (owner % nq) * nz + owner // nq).astype(F32)
            slots = jnp.transpose((row == slot_ref[k : k + 1, :]).astype(F32))
        else:
            hot_t = (row == q * nz + z).astype(F32)
            slots = (lane == row).astype(F32)
        owner_hot[rows, :] = jnp.transpose(hot_t).astype(BF16)
        owner_hot_t[:, rows] = hot_t[0 : owner_hot_t.shape[0], :].astype(BF16)
        slot_hot[rows, :] = slots

    def wide(line):
        return jnp.transpose(jnp.broadcast_to(line, (LANES, atoms)))

    def block_rows(p):
        return pl.ds(pl.multiple_of(p * atoms, atoms), atoms)

    def widen(p, carry):
        rows = block_rows(p)
        wide_x[rows, :] = wide(qm_all[p, 0:1, :])
        wide_y[rows, :] = wide(qm_all[p, 1:2, :])
        wide_z[rows, :] = wide(qm_all[p, 2:3, :])
        pot_q[q, pl.ds(nz + p, 1), :] = qm_all[p, 3:4, :]
        return carry

    def chunk_columns(p):
        return pl.ds(pl.multiple_of(p * mm_tiles * LANES, LANES), mm_tiles * LANES)

    def stacked(place, norm_first, order):
        norm = jnp.sum(place * place, axis=0, keepdims=True)
        one, nothing = jnp.ones_like(norm), jnp.zeros((3, norm.shape[1]), F32)
        if norm_first:
            record = jnp.concatenate([place, norm, one, nothing], axis=0)
        else:
            record = jnp.concatenate([-2.0 * place, one, norm + SOFTEN, nothing], axis=0)
        pieces = [piece.astype(F32) for piece in split3(record)]
        return jnp.concatenate([pieces[k] for k in order], axis=0)

    def take_charges(p):
        where = chunk_columns(p)
        mm_parts[:, where] = stacked(mm_all[p, 0:3, :], True, (0, 1, 0, 1, 2, 0)).astype(BF16)
        charges[:, where] = mm_all[p, 3:4, :]

    take_charges(q)
    each(plane, lambda d: take_charges(wait_from(MM_Q, plane, d, mm_all)))

    def potential_block(d):
        p = jnp.where(d > 0, near[5](near[3](d)), z)
        rows = block_rows(p)
        parts = stacked(qm_all[p, 0:3, :], False, (0, 0, 1, 1, 0, 2))
        parts = jnp.concatenate([parts, jnp.zeros((LANES - 48, atoms), F32)], axis=0)
        parts = jnp.transpose(parts).astype(BF16)
        square = jnp.dot(parts[:, 0:48], mm_parts[...], preferred_element_type=F32)
        inverse = lax.rsqrt(square)
        inverses[rows, :] = inverse
        term = inverse * charges[...]
        running = term[:, 0:LANES]
        for t in range(1, nq * mm_tiles):
            running = running + term[:, t * LANES : (t + 1) * LANES]
        pot_x[x, pl.ds(p, 1), :] = jnp.sum(jnp.transpose(running), axis=0, keepdims=True)

    def potential_step(d, carry):
        @pl.when(d > 0)
        def _():
            wait_from(QM_N, near, d, qm_all)

        potential_block(d)
        return carry

    lax.fori_loop(0, nz, potential_step, 0)

    def columns(chunk):
        return [
            [mm_all[chunk, c : c + 1, t * LANES : (t + 1) * LANES] for c in range(4)]
            for t in range(mm_tiles)
        ]

    def lines(acc, p):
        return jnp.sum(jnp.transpose(acc[block_rows(p), :]), axis=0, keepdims=True)

    send_all(POT_X, row_x, lambda p: pot_x.at[x], pot_x)
    acc_x[...] = jnp.zeros_like(acc_x)
    acc_y[...] = jnp.zeros_like(acc_y)
    acc_z[...] = jnp.zeros_like(acc_z)
    lax.fori_loop(0, nz, widen, 0)
    qm_lines[0:1, :] = jnp.ones((1, nz * atoms), F32)
    for p in range(nz):
        qm_lines[1:4, p * atoms : (p + 1) * atoms] = qm_all[p, 0:3, :]
    qm_lines[4:8, :] = jnp.zeros((4, nz * atoms), F32)

    def pull_chunk(chunk, carry):
        tiles = columns(chunk)

        def group(g, inner):
            rows = pl.ds(pl.multiple_of(g * FORCE_ROWS, FORCE_ROWS), FORCE_ROWS)
            px, py, pz = wide_x[rows, :], wide_y[rows, :], wide_z[rows, :]
            fx, fy, fz = acc_x[rows, :], acc_y[rows, :], acc_z[rows, :]
            for t, (mx, my, mz, mq) in enumerate(tiles):
                where = pl.ds(pl.multiple_of((chunk * mm_tiles + t) * LANES, LANES), LANES)
                inverse = inverses[rows, where]
                cube = inverse * inverse * inverse
                inverses[rows, where] = cube
                pull = cube * mq
                fx = fx + pull * (px - mx)
                fy = fy + pull * (py - my)
                fz = fz + pull * (pz - mz)
            acc_x[rows, :], acc_y[rows, :], acc_z[rows, :] = fx, fy, fz
            return inner

        return lax.fori_loop(0, nz * atoms // FORCE_ROWS, group, carry)

    early = min(EARLY, nq)
    lax.fori_loop(0, early, pull_chunk, 0)
    wait_all(POT_X, row_x, pot_x)
    pot_z[ring] = total(pot_x, nx)
    send_all(POT_Z, far, lambda p: pot_z.at[ring], pot_z)
    lax.fori_loop(early, nq, pull_chunk, 0)

    def gather_force(p, carry):
        qmf_mine[p, 0:1, :] = lines(acc_x, p)
        qmf_mine[p, 1:2, :] = lines(acc_y, p)
        qmf_mine[p, 2:3, :] = lines(acc_z, p)
        return carry

    lax.fori_loop(0, nz, gather_force, 0)
    qmf_z[ring] = qmf_mine[z]
    wait_all(POT_Z, far, pot_z)
    pot_q[q, 0:nz, :] = total(pot_z, rings) * coupling
    send_all(POT_Q, plane, lambda p: pot_q.at[q], pot_q)
    send_all(QMF_Z, far, lambda p: qmf_mine.at[p % nz], qmf_z)
    wait_all(POT_Q, plane, pot_q)

    potentials = jnp.concatenate([pot_q[p, 0:nz, :] for p in range(nq)], axis=0)
    codes = jnp.concatenate([pot_q[p, nz : 2 * nz, :] for p in range(nq)], axis=0)
    gain = gain_ref[...]
    table = table_wide[...].astype(BF16)
    pieces = [*split3(potentials), codes.astype(BF16)]
    neighbour = jnp.zeros((atoms, LANES), F32)
    for k in range(neighbours + 1):
        rows = slice(k * atoms, (k + 1) * atoms)
        hot = owner_hot[rows, 0:blocks]
        slots = slot_hot[rows, :]
        picked = [jnp.dot(hot, piece, preferred_element_type=F32) for piece in pieces]
        potential = jnp.sum((picked[0] + picked[1] + picked[2]) * slots, axis=1, keepdims=True)
        code = jnp.sum(picked[3] * slots, axis=1, keepdims=True)
        live = (code >= 0).astype(F32)
        kinds = (lane.astype(F32) == code).astype(F32).astype(BF16)
        base = jnp.dot(kinds, table, preferred_element_type=F32)
        start = (live * (base + potential * gain)).astype(BF16)
        if k < neighbours:
            neighbour = neighbour + start.astype(F32)
    mixed = start.astype(F32) + jnp.dot(
        neighbour.astype(BF16), message_ref[...], preferred_element_type=F32
    )
    before = jnp.dot(mixed.astype(BF16), hidden_ref[...], preferred_element_type=F32)
    sigma = jax.nn.sigmoid(before)
    active = before * sigma
    charge_part = live * jnp.sum(active * readout_ref[...], axis=1, keepdims=True)
    back_active = live * (energy_ref[...] + potential * readout_ref[...])
    back_before = (back_active * sigma * (1.0 + before * (1.0 - sigma))).astype(BF16)
    nt = (((1,), (1,)), ((), ()))
    back_mixed = lax.dot_general(back_before, hidden_ref[...], nt, preferred_element_type=F32)
    back_sum = lax.dot_general(
        back_mixed.astype(BF16), message_ref[...], nt, preferred_element_type=F32
    ).astype(BF16)
    out_going = jnp.sum(back_sum.astype(F32) * gain, axis=1, keepdims=True)
    staying = jnp.sum(back_mixed * gain, axis=1, keepdims=True) + charge_part
    spread = jnp.zeros((blocks, LANES), F32)
    parts_out, parts_stay = split3(out_going), split3(staying)
    for k in range(neighbours + 1):
        rows = slice(k * atoms, (k + 1) * atoms)
        slots = slot_hot[rows, :]
        for part in parts_out if k < neighbours else parts_stay:
            spread = spread + jnp.dot(
                owner_hot_t[0:blocks, rows],
                (slots * part.astype(F32)).astype(BF16),
                preferred_element_type=F32,
            )
    for p in range(nq):
        grad_mine[p] = spread[p * nz : (p + 1) * nz, :]
    send_all(GRAD_Q, plane, lambda p: grad_mine.at[p], grad_q)
    grad_q[q] = grad_mine[q]
    energy_part = live * jnp.sum(active * energy_ref[...], axis=1, keepdims=True)
    atom_energy = energy_part + charge_part * potential
    atom_energy_ref[...] = jnp.sum(
        jnp.where(lane == row, atom_energy, 0.0), axis=0, keepdims=True
    )
    wait_all(GRAD_Q, plane, grad_q)
    grad_n[z] = total(grad_q, nq)
    send_all(GRAD_N, near, lambda p: grad_n.at[z], grad_n)
    wait_all(QMF_Z, far, qmf_z)
    qmf_x[x] = total(qmf_z, rings)
    send_all(QMF_X, row_x, lambda p: qmf_x.at[x], qmf_x)
    wait_all(GRAD_N, near, grad_n)
    live_plane = (pot_q[q, nz : 2 * nz, :] >= 0).astype(F32)
    grad_sum[...] = live_plane * total(grad_n, nz)

    effective = jnp.concatenate([grad_sum[p : p + 1, :] for p in range(nz)], axis=1)
    weights = qm_lines[...] * effective
    high = weights.astype(BF16).astype(F32)
    weights = jnp.concatenate([high, weights - high], axis=0).astype(BF16)

    def push_chunk(step, carry):
        d = nq - step
        chunk = jnp.where(d > 0, plane[2](d), q)

        cube = inverses[:, chunk_columns(chunk)]
        high = cube.astype(BF16)
        low = (cube - high.astype(F32)).astype(BF16)
        sums = jnp.dot(weights, high, preferred_element_type=F32)
        sums = sums + jnp.dot(weights, low, preferred_element_type=F32)
        sums = sums[0:8, :] + sums[8:16, :]
        mmf_mine[chunk] = sums[1:4, :] - sums[0:1, :] * mm_all[chunk, 0:3, :]

        @pl.when(d > 0)
        def _():
            outgoing(MMF_Q, plane, lambda p: mmf_mine.at[p], mmf_q, d).start()

        return carry

    lax.fori_loop(1, nq + 1, push_chunk, 0)
    mmf_q[q] = mmf_mine[q]
    sent_all(QM_N, near, lambda p: qm_all.at[z], qm_all)
    sent_all(MM_Q, plane, lambda p: mm_all.at[q], mm_all)
    sent_all(POT_X, row_x, lambda p: pot_x.at[x], pot_x)
    sent_all(POT_Z, far, lambda p: pot_z.at[ring], pot_z)
    sent_all(POT_Q, plane, lambda p: pot_q.at[q], pot_q)
    sent_all(QMF_Z, far, lambda p: qmf_mine.at[p % nz], qmf_z)
    sent_all(GRAD_Q, plane, lambda p: grad_mine.at[p], grad_q)
    sent_all(GRAD_N, near, lambda p: grad_n.at[z], grad_n)
    wait_all(QMF_X, row_x, qmf_x)
    qm_force_ref[...] = total(qmf_x, nx) * (grad_sum[pl.ds(z, 1), :] * coupling)
    sent_all(QMF_X, row_x, lambda p: qmf_x.at[x], qmf_x)
    sent_all(MMF_Q, plane, lambda p: mmf_mine.at[p], mmf_q)
    wait_all(MMF_Q, plane, mmf_q)
    mm_force_ref[...] = total(mmf_q, nq) * (charge_ref[...] * -coupling)


def on_device(
    nz,
    nq,
    nr,
    qm_pos,
    species,
    qm_count,
    ghost_owner,
    ghost_slot,
    mm_pos,
    mm_charge,
    species_table,
    potential_gain,
    message_weight,
    hidden_weight,
    energy_readout,
    charge_readout,
):
    atoms = qm_pos.shape[1]
    mm_here = mm_pos.shape[1]
    nx = nr // 2
    coupling = float(mm_here * nz * nq * nr) ** (-0.5)
    here = nz * atoms
    groups = ghost_owner.shape[1] + 1
    hot_rows = -(-nz * nq // 16) * 16
    small = lambda *shape: pltpu.VMEM(shape, F32)
    vmem = pl.BlockSpec(memory_space=pltpu.VMEM)
    atom_energy, qm_force, mm_force = pl.pallas_call(
        functools.partial(kernel, nz, nq, nx, coupling),
        out_shape=(
            jax.ShapeDtypeStruct((1, atoms), F32),
            jax.ShapeDtypeStruct((3, atoms), F32),
            jax.ShapeDtypeStruct((3, mm_here), F32),
        ),
        in_specs=[vmem] * 13,
        out_specs=(vmem,) * 3,
        scratch_shapes=[
            small(nq, 4, mm_here),
            small(nz, 4, atoms),
            small(nx, nz, atoms),
            small(2 * nz, nz, atoms),
            small(nq, 2 * nz, atoms),
            small(nq, nz, atoms),
            small(nq, nz, atoms),
            small(nz, nz, atoms),
            small(nz, atoms),
            small(nz, 3, atoms),
            small(2 * nz, 3, atoms),
            small(nx, 3, atoms),
            small(nq, 3, mm_here),
            small(nq, 3, mm_here),
            *[small(here, LANES)] * 6,
            small(here, nq * mm_here),
            pltpu.VMEM((here, LANES), BF16),
            pltpu.VMEM((48, nq * mm_here), BF16),
            small(1, nq * mm_here),
            small(8, here),
            small(LANES, LANES),
            pltpu.VMEM((groups * atoms, LANES), BF16),
            pltpu.VMEM((hot_rows, groups * atoms), BF16),
            small(groups * atoms, LANES),
            pltpu.SemaphoreType.DMA((10, max(2 * nz, nq, nx))),
            pltpu.SemaphoreType.DMA((10, max(2 * nz, nq, nx))),
        ],
        compiler_params=pltpu.CompilerParams(
            collective_id=0, has_side_effects=True, vmem_limit_bytes=48 * 2**20
        ),
    )(
        qm_pos,
        species[None, :],
        qm_count[None, :],
        ghost_owner.T,
        ghost_slot.T,
        mm_pos,
        mm_charge[None, :],
        species_table,
        potential_gain[None, :],
        message_weight,
        hidden_weight,
        energy_readout[None, :],
        charge_readout[None, :],
    )
    return (atom_energy[0], qm_force, mm_force)


def solution(mesh):
    blocks, nr = mesh.shape["blk"], mesh.shape["rep"]
    nq = min(8, blocks // 2)
    placed = (
        P(None, "blk"),
        P("blk"),
        P("blk"),
        P("blk", None),
        P("blk", None),
        P(None, ("blk", "rep")),
        P(("blk", "rep")),
        P(),
        P(),
        P(),
        P(),
        P(),
        P(),
    )
    return jax.shard_map(
        functools.partial(on_device, blocks // nq, nq, nr),
        mesh=mesh,
        in_specs=placed,
        out_specs=(P("blk"), P(None, "blk"), P(None, ("blk", "rep"))),
        check_vma=False,
    )
```

```python
import functools

import jax
import jax.numpy as jnp
from jax import lax
from jax.experimental import pallas as pl
from jax.experimental.pallas import tpu as pltpu
from jax.sharding import PartitionSpec as P

SOFTEN = 0.25
LANES = 128
FORCE_ROWS = 32
EARLY = 2
TABLE = 7
MESH = pl.DeviceIdType.MESH
F32 = jnp.float32
BF16 = jnp.bfloat16

QM_N, MM_Q, POT_X, POT_Z, POT_Q, GRAD_Q, GRAD_N, QMF_Z, QMF_X, MMF_Q = range(10)


def split3(value):
    high = value.astype(BF16)
    rest = value - high.astype(F32)
    middle = rest.astype(BF16)
    low = (rest - middle.astype(F32)).astype(BF16)
    return high, middle, low


def kernel(
    nz,
    nq,
    nx,
    coupling,
    qm_hbm,
    species_hbm,
    count_hbm,
    owner_hbm,
    slot_hbm,
    mm_hbm,
    charge_hbm,
    table_ref,
    gain_hbm,
    message_hbm,
    hidden_hbm,
    energy_hbm,
    readout_hbm,
    atom_energy_ref,
    qm_force_ref,
    mm_force_ref,
    mm_all,
    qm_all,
    pot_x,
    pot_z,
    pot_q,
    grad_mine,
    grad_q,
    grad_n,
    grad_sum,
    qmf_mine,
    qmf_z,
    qmf_x,
    mmf_mine,
    mmf_q,
    wide_x,
    wide_y,
    wide_z,
    acc_x,
    acc_y,
    acc_z,
    inverses,
    mm_parts,
    charges,
    qm_lines,
    table_wide,
    owner_hot,
    owner_hot_t,
    slot_hot,
    qm_ref,
    species_ref,
    count_ref,
    owner_ref,
    slot_ref,
    mm_ref,
    charge_ref,
    gain_ref,
    message_ref,
    hidden_ref,
    energy_ref,
    readout_ref,
    fetch_sems,
    send_sems,
    recv_sems,
):
    blk = lax.axis_index("blk")
    rep = lax.axis_index("rep")
    z, q = blk // nq, blk % nq
    x, ring = rep // 2, (rep % 2) * nz + z
    rings = 2 * nz
    atoms = qm_ref.shape[1]
    mm_tiles = mm_ref.shape[1] // LANES
    blocks = nz * nq
    neighbours = owner_ref.shape[0]

    def at_ring(p):
        return ((p % nz) * nq + q, x * 2 + p // nz)

    def at_q(p):
        return (z * nq + p, rep)

    def shift(d):
        return (d + 1) // 2 * (2 * (d % 2) - 1)

    def q_place(d, sign):
        y = (q // 2 + (nq // 2) + sign * (d // 2)) % (nq // 2)
        return y * 2 + (q + d) % 2

    same = lambda p: p
    near = (nz, ring, lambda d: (ring + rings - shift(d)) % rings, lambda d: (ring + rings + shift(d)) % rings, at_ring, lambda p: p % nz)
    far = (rings, ring, lambda d: (ring + d) % rings, lambda d: (ring + rings - d) % rings, at_ring, same)
    plane = (nq, q, lambda d: q_place(d, 1), lambda d: q_place(d, -1), at_q, same)
    row_x = (nx, x, lambda d: (x + d) % nx, lambda d: (x + nx - d) % nx, lambda p: (blk, p * 2 + rep % 2), same)

    def copy_to(stage, d, device, src, dst):
        return pltpu.make_async_remote_copy(
            src_ref=src,
            dst_ref=dst,
            send_sem=send_sems.at[stage, d],
            recv_sem=recv_sems.at[stage, d],
            device_id=device,
            device_id_type=MESH,
        )

    def each(axis, step):
        def body(d, carry):
            step(d)
            return carry

        lax.fori_loop(1, axis[0], body, 0)

    def outgoing(stage, axis, src_of, buffer, d):
        _, mine, to, _, device, slot = axis
        p = to(d)
        return copy_to(stage, d, device(p), src_of(p), buffer.at[slot(mine)])

    def send_all(stage, axis, src_of, buffer):
        each(axis, lambda d: outgoing(stage, axis, src_of, buffer, d).start())

    def sent_all(stage, axis, src_of, buffer):
        each(axis, lambda d: outgoing(stage, axis, src_of, buffer, d).wait_send())

    def wait_from(stage, axis, d, buffer):
        _, _, _, came, device, slot = axis
        p = came(d)
        place = buffer.at[slot(p)]
        copy_to(stage, d, device(p), place, place).wait_recv()
        return slot(p)

    def wait_all(stage, axis, buffer):
        def step(d):
            wait_from(stage, axis, d, buffer)

        each(axis, step)

    def total(buffer, size):
        result = buffer[0]
        for p in range(1, size):
            result = result + buffer[p]
        return result

    fetches = [
        pltpu.make_async_copy(src, dst, fetch_sems.at[k])
        for k, (src, dst) in enumerate(
            [
                (mm_hbm, mm_ref),
                (charge_hbm, charge_ref),
                (qm_hbm, qm_ref),
                (species_hbm, species_ref),
                (count_hbm, count_ref),
                (owner_hbm, owner_ref),
                (slot_hbm, slot_ref),
                (gain_hbm, gain_ref),
                (message_hbm, message_ref),
                (hidden_hbm, hidden_ref),
                (energy_hbm, energy_ref),
                (readout_hbm, readout_ref),
            ]
        )
    ]
    for fetch in fetches:
        fetch.start()

    barrier = pltpu.get_barrier_semaphore()
    def greet(device):
        pl.semaphore_signal(barrier, inc=1, device_id=device, device_id_type=MESH)

    def greet_ring(d, carry):
        greet(at_ring((ring + d) % rings))
        greet(at_ring((ring + rings - d) % rings))
        return carry

    lax.fori_loop(1, nz // 2 + 1, greet_ring, 0)
    each(plane, lambda d: greet(at_q(plane[2](d))))
    each(row_x, lambda d: greet(row_x[4](row_x[2](d))))
    for fetch in fetches[:5]:
        fetch.wait()

    mm_all[q, 0:3, :] = mm_ref[...]
    mm_all[q, 3:4, :] = charge_ref[...]
    live_row = lax.broadcasted_iota(jnp.int32, (1, atoms), 1) < count_ref[...]
    qm_all[z, 0:3, :] = qm_ref[...]
    qm_all[z, 3:4, :] = jnp.where(live_row, species_ref[...], -1).astype(F32)

    pl.semaphore_wait(barrier, nz + nq + nx - 2)
    send_all(QM_N, near, lambda p: qm_all.at[z], qm_all)
    send_all(MM_Q, plane, lambda p: mm_all.at[q], mm_all)

    for fetch in fetches[5:]:
        fetch.wait()
    table_wide[...] = jnp.zeros_like(table_wide)
    table_wide[0 : table_ref.shape[0], :] = table_ref[...].astype(F32)
    lane = lax.broadcasted_iota(jnp.int32, (atoms, LANES), 1)
    row = lax.broadcasted_iota(jnp.int32, (atoms, LANES), 0)
    for k in range(neighbours + 1):
        rows = slice(k * atoms, (k + 1) * atoms)
        if k < neighbours:
            owner = owner_ref[k : k + 1, :]
            hot_t = (row == (owner % nq) * nz + owner // nq).astype(F32)
            slots = jnp.transpose((row == slot_ref[k : k + 1, :]).astype(F32))
        else:
            hot_t = (row == q * nz + z).astype(F32)
            slots = (lane == row).astype(F32)
        owner_hot[rows, :] = jnp.transpose(hot_t).astype(BF16)
        owner_hot_t[:, rows] = hot_t[0 : owner_hot_t.shape[0], :].astype(BF16)
        slot_hot[rows, :] = slots

    def wide(line):
        return jnp.transpose(jnp.broadcast_to(line, (LANES, atoms)))

    def block_rows(p):
        return pl.ds(pl.multiple_of(p * atoms, atoms), atoms)

    def widen(p, carry):
        rows = block_rows(p)
        wide_x[rows, :] = wide(qm_all[p, 0:1, :])
        wide_y[rows, :] = wide(qm_all[p, 1:2, :])
        wide_z[rows, :] = wide(qm_all[p, 2:3, :])
        pot_q[q, pl.ds(nz + p, 1), :] = qm_all[p, 3:4, :]
        return carry

    def chunk_columns(p):
        return pl.ds(pl.multiple_of(p * mm_tiles * LANES, LANES), mm_tiles * LANES)

    def stacked(place, norm_first, order):
        norm = jnp.sum(place * place, axis=0, keepdims=True)
        one, nothing = jnp.ones_like(norm), jnp.zeros((3, norm.shape[1]), F32)
        if norm_first:
            record = jnp.concatenate([place, norm, one, nothing], axis=0)
        else:
            record = jnp.concatenate([-2.0 * place, one, norm + SOFTEN, nothing], axis=0)
        pieces = [piece.astype(F32) for piece in split3(record)]
        return jnp.concatenate([pieces[k] for k in order], axis=0)

    def take_charges(p):
        where = chunk_columns(p)
        mm_parts[:, where] = stacked(mm_all[p, 0:3, :], True, (0, 1, 0, 1, 2, 0)).astype(BF16)
        charges[:, where] = mm_all[p, 3:4, :]

    take_charges(q)
    each(plane, lambda d: take_charges(wait_from(MM_Q, plane, d, mm_all)))

    def take_block(p):
        parts = stacked(qm_all[p, 0:3, :], False, (0, 0, 1, 1, 0, 2))
        parts = jnp.concatenate([parts, jnp.zeros((LANES - 48, atoms), F32)], axis=0)
        return jnp.transpose(parts).astype(BF16)[:, 0:48]

    def potential_step(k, carry):
        @pl.when(k > 0)
        def _():
            wait_from(QM_N, near, 2 * k, qm_all)

        wait_from(QM_N, near, 2 * k + 1, qm_all)
        pair = [jnp.where(k > 0, near[5](near[3](2 * k)), z), near[5](near[3](2 * k + 1))]
        parts = jnp.concatenate([take_block(p) for p in pair], axis=0)
        square = jnp.dot(parts, mm_parts[...], preferred_element_type=F32)
        inverse = lax.rsqrt(square)
        term = inverse * charges[...]
        running = term[:, 0:LANES]
        for t in range(1, nq * mm_tiles):
            running = running + term[:, t * LANES : (t + 1) * LANES]
        for k, p in enumerate(pair):
            rows = slice(k * atoms, (k + 1) * atoms)
            inverses[block_rows(p), :] = inverse[rows, :]
            pot_x[x, pl.ds(p, 1), :] = jnp.sum(jnp.transpose(running[rows, :]), axis=0, keepdims=True)
        return carry

    lax.fori_loop(0, nz // 2, potential_step, 0)

    def columns(chunk):
        return [
            [mm_all[chunk, c : c + 1, t * LANES : (t + 1) * LANES] for c in range(4)]
            for t in range(mm_tiles)
        ]

    def lines(acc, p):
        return jnp.sum(jnp.transpose(acc[block_rows(p), :]), axis=0, keepdims=True)

    send_all(POT_X, row_x, lambda p: pot_x.at[x], pot_x)
    acc_x[...] = jnp.zeros_like(acc_x)
    acc_y[...] = jnp.zeros_like(acc_y)
    acc_z[...] = jnp.zeros_like(acc_z)
    lax.fori_loop(0, nz, widen, 0)
    qm_lines[0:1, :] = jnp.ones((1, nz * atoms), F32)
    for p in range(nz):
        qm_lines[1:4, p * atoms : (p + 1) * atoms] = qm_all[p, 0:3, :]
    qm_lines[4:8, :] = jnp.zeros((4, nz * atoms), F32)

    def pull_chunk(chunk, carry):
        tiles = columns(chunk)

        def group(g, inner):
            rows = pl.ds(pl.multiple_of(g * FORCE_ROWS, FORCE_ROWS), FORCE_ROWS)
            px, py, pz = wide_x[rows, :], wide_y[rows, :], wide_z[rows, :]
            fx, fy, fz = acc_x[rows, :], acc_y[rows, :], acc_z[rows, :]
            for t, (mx, my, mz, mq) in enumerate(tiles):
                where = pl.ds(pl.multiple_of((chunk * mm_tiles + t) * LANES, LANES), LANES)
                inverse = inverses[rows, where]
                cube = inverse * inverse * inverse
                inverses[rows, where] = cube
                pull = cube * mq
                fx = fx + pull * (px - mx)
                fy = fy + pull * (py - my)
                fz = fz + pull * (pz - mz)
            acc_x[rows, :], acc_y[rows, :], acc_z[rows, :] = fx, fy, fz
            return inner

        return lax.fori_loop(0, nz * atoms // FORCE_ROWS, group, carry)

    early = min(EARLY, nq)
    lax.fori_loop(0, early, pull_chunk, 0)
    wait_all(POT_X, row_x, pot_x)
    pot_z[ring] = total(pot_x, nx)
    send_all(POT_Z, far, lambda p: pot_z.at[ring], pot_z)
    lax.fori_loop(early, nq, pull_chunk, 0)

    wait_all(POT_Z, far, pot_z)
    pot_q[q, 0:nz, :] = total(pot_z, rings) * coupling
    send_all(POT_Q, plane, lambda p: pot_q.at[q], pot_q)
    def gather_force(p, carry):
        qmf_mine[p, 0:1, :] = lines(acc_x, p)
        qmf_mine[p, 1:2, :] = lines(acc_y, p)
        qmf_mine[p, 2:3, :] = lines(acc_z, p)
        return carry

    lax.fori_loop(0, nz, gather_force, 0)
    qmf_z[ring] = qmf_mine[z]
    send_all(QMF_Z, far, lambda p: qmf_mine.at[p % nz], qmf_z)
    wait_all(POT_Q, plane, pot_q)

    potentials = jnp.concatenate([pot_q[p, 0:nz, :] for p in range(nq)], axis=0)
    codes = jnp.concatenate([pot_q[p, nz : 2 * nz, :] for p in range(nq)], axis=0)
    gain = gain_ref[...]
    table = table_wide[...].astype(BF16)
    pieces = [*split3(potentials), codes.astype(BF16)]
    neighbour = jnp.zeros((atoms, LANES), F32)
    for k in range(neighbours + 1):
        rows = slice(k * atoms, (k + 1) * atoms)
        hot = owner_hot[rows, 0:blocks]
        slots = slot_hot[rows, :]
        picked = [jnp.dot(hot, piece, preferred_element_type=F32) for piece in pieces]
        potential = jnp.sum((picked[0] + picked[1] + picked[2]) * slots, axis=1, keepdims=True)
        code = jnp.sum(picked[3] * slots, axis=1, keepdims=True)
        live = (code >= 0).astype(F32)
        kinds = (lane.astype(F32) == code).astype(F32).astype(BF16)
        base = jnp.dot(kinds, table, preferred_element_type=F32)
        start = (live * (base + potential * gain)).astype(BF16)
        if k < neighbours:
            neighbour = neighbour + start.astype(F32)
    mixed = start.astype(F32) + jnp.dot(
        neighbour.astype(BF16), message_ref[...], preferred_element_type=F32
    )
    before = jnp.dot(mixed.astype(BF16), hidden_ref[...], preferred_element_type=F32)
    sigma = jax.nn.sigmoid(before)
    active = before * sigma
    charge_part = live * jnp.sum(active * readout_ref[...], axis=1, keepdims=True)
    back_active = live * (energy_ref[...] + potential * readout_ref[...])
    back_before = (back_active * sigma * (1.0 + before * (1.0 - sigma))).astype(BF16)
    nt = (((1,), (1,)), ((), ()))
    back_mixed = lax.dot_general(back_before, hidden_ref[...], nt, preferred_element_type=F32)
    back_sum = lax.dot_general(
        back_mixed.astype(BF16), message_ref[...], nt, preferred_element_type=F32
    ).astype(BF16)
    out_going = jnp.sum(back_sum.astype(F32) * gain, axis=1, keepdims=True)
    staying = jnp.sum(back_mixed * gain, axis=1, keepdims=True) + charge_part
    spread = jnp.zeros((blocks, LANES), F32)
    parts_out, parts_stay = split3(out_going), split3(staying)
    for k in range(neighbours + 1):
        rows = slice(k * atoms, (k + 1) * atoms)
        slots = slot_hot[rows, :]
        for part in parts_out if k < neighbours else parts_stay:
            spread = spread + jnp.dot(
                owner_hot_t[0:blocks, rows],
                (slots * part.astype(F32)).astype(BF16),
                preferred_element_type=F32,
            )
    for p in range(nq):
        grad_mine[p] = spread[p * nz : (p + 1) * nz, :]
    send_all(GRAD_Q, plane, lambda p: grad_mine.at[p], grad_q)
    grad_q[q] = grad_mine[q]
    energy_part = live * jnp.sum(active * energy_ref[...], axis=1, keepdims=True)
    atom_energy = energy_part + charge_part * potential
    atom_energy_ref[...] = jnp.sum(
        jnp.where(lane == row, atom_energy, 0.0), axis=0, keepdims=True
    )
    wait_all(GRAD_Q, plane, grad_q)
    grad_n[z] = total(grad_q, nq)
    send_all(GRAD_N, near, lambda p: grad_n.at[z], grad_n)
    wait_all(QMF_Z, far, qmf_z)
    qmf_x[x] = total(qmf_z, rings)
    send_all(QMF_X, row_x, lambda p: qmf_x.at[x], qmf_x)
    wait_all(GRAD_N, near, grad_n)
    live_plane = (pot_q[q, nz : 2 * nz, :] >= 0).astype(F32)
    grad_sum[...] = live_plane * total(grad_n, nz)

    effective = jnp.concatenate([grad_sum[p : p + 1, :] for p in range(nz)], axis=1)
    weights = qm_lines[...] * effective
    high = weights.astype(BF16).astype(F32)
    weights = jnp.concatenate([high, weights - high], axis=0).astype(BF16)

    def push_chunk(step, carry):
        d = nq - step
        chunk = jnp.where(d > 0, plane[2](d), q)

        cube = inverses[:, chunk_columns(chunk)]
        high = cube.astype(BF16)
        low = (cube - high.astype(F32)).astype(BF16)
        sums = jnp.dot(weights, high, preferred_element_type=F32)
        sums = sums + jnp.dot(weights, low, preferred_element_type=F32)
        sums = sums[0:8, :] + sums[8:16, :]
        mmf_mine[chunk] = sums[1:4, :] - sums[0:1, :] * mm_all[chunk, 0:3, :]

        @pl.when(d > 0)
        def _():
            outgoing(MMF_Q, plane, lambda p: mmf_mine.at[p], mmf_q, d).start()

        return carry

    lax.fori_loop(1, nq + 1, push_chunk, 0)
    mmf_q[q] = mmf_mine[q]
    sent_all(QM_N, near, lambda p: qm_all.at[z], qm_all)
    sent_all(MM_Q, plane, lambda p: mm_all.at[q], mm_all)
    sent_all(POT_X, row_x, lambda p: pot_x.at[x], pot_x)
    sent_all(POT_Z, far, lambda p: pot_z.at[ring], pot_z)
    sent_all(POT_Q, plane, lambda p: pot_q.at[q], pot_q)
    sent_all(QMF_Z, far, lambda p: qmf_mine.at[p % nz], qmf_z)
    sent_all(GRAD_Q, plane, lambda p: grad_mine.at[p], grad_q)
    sent_all(GRAD_N, near, lambda p: grad_n.at[z], grad_n)
    wait_all(QMF_X, row_x, qmf_x)
    qm_force_ref[...] = total(qmf_x, nx) * (grad_sum[pl.ds(z, 1), :] * coupling)
    sent_all(QMF_X, row_x, lambda p: qmf_x.at[x], qmf_x)
    sent_all(MMF_Q, plane, lambda p: mmf_mine.at[p], mmf_q)
    wait_all(MMF_Q, plane, mmf_q)
    mm_force_ref[...] = total(mmf_q, nq) * (charge_ref[...] * -coupling)


def on_device(
    nz,
    nq,
    nr,
    qm_pos,
    species,
    qm_count,
    ghost_owner,
    ghost_slot,
    mm_pos,
    mm_charge,
    species_table,
    potential_gain,
    message_weight,
    hidden_weight,
    energy_readout,
    charge_readout,
):
    atoms = qm_pos.shape[1]
    mm_here = mm_pos.shape[1]
    nx = nr // 2
    coupling = float(mm_here * nz * nq * nr) ** (-0.5)
    here = nz * atoms
    groups = ghost_owner.shape[1] + 1
    hot_rows = -(-nz * nq // 16) * 16
    arguments = (
        qm_pos,
        species[None, :],
        qm_count[None, :],
        ghost_owner.T,
        ghost_slot.T,
        mm_pos,
        mm_charge[None, :],
        species_table,
        potential_gain[None, :],
        message_weight,
        hidden_weight,
        energy_readout[None, :],
        charge_readout[None, :],
    )
    small = lambda *shape: pltpu.VMEM(shape, F32)
    vmem = pl.BlockSpec(memory_space=pltpu.VMEM)
    hbm = pl.BlockSpec(memory_space=pltpu.HBM)
    atom_energy, qm_force, mm_force = pl.pallas_call(
        functools.partial(kernel, nz, nq, nx, coupling),
        out_shape=(
            jax.ShapeDtypeStruct((1, atoms), F32),
            jax.ShapeDtypeStruct((3, atoms), F32),
            jax.ShapeDtypeStruct((3, mm_here), F32),
        ),
        in_specs=[hbm] * 7 + [vmem] + [hbm] * 5,
        out_specs=(vmem,) * 3,
        scratch_shapes=[
            small(nq, 4, mm_here),
            small(nz, 4, atoms),
            small(nx, nz, atoms),
            small(2 * nz, nz, atoms),
            small(nq, 2 * nz, atoms),
            small(nq, nz, atoms),
            small(nq, nz, atoms),
            small(nz, nz, atoms),
            small(nz, atoms),
            small(nz, 3, atoms),
            small(2 * nz, 3, atoms),
            small(nx, 3, atoms),
            small(nq, 3, mm_here),
            small(nq, 3, mm_here),
            *[small(here, LANES)] * 6,
            small(here, nq * mm_here),
            pltpu.VMEM((48, nq * mm_here), BF16),
            small(1, nq * mm_here),
            small(8, here),
            small(LANES, LANES),
            pltpu.VMEM((groups * atoms, LANES), BF16),
            pltpu.VMEM((hot_rows, groups * atoms), BF16),
            small(groups * atoms, LANES),
            *[pltpu.VMEM(a.shape, a.dtype) for k, a in enumerate(arguments) if k != TABLE],
            pltpu.SemaphoreType.DMA((12,)),
            pltpu.SemaphoreType.DMA((10, max(2 * nz, nq, nx))),
            pltpu.SemaphoreType.DMA((10, max(2 * nz, nq, nx))),
        ],
        compiler_params=pltpu.CompilerParams(
            collective_id=0, has_side_effects=True, vmem_limit_bytes=56 * 2**20
        ),
    )(*arguments)
    return (atom_energy[0], qm_force, mm_force)


def solution(mesh):
    blocks, nr = mesh.shape["blk"], mesh.shape["rep"]
    nq = min(8, blocks // 2)
    placed = (
        P(None, "blk"),
        P("blk"),
        P("blk"),
        P("blk", None),
        P("blk", None),
        P(None, ("blk", "rep")),
        P(("blk", "rep")),
        P(),
        P(),
        P(),
        P(),
        P(),
        P(),
    )
    return jax.shard_map(
        functools.partial(on_device, blocks // nq, nq, nr),
        mesh=mesh,
        in_specs=placed,
        out_specs=(P("blk"), P(None, "blk"), P(None, ("blk", "rep"))),
        check_vma=False,
    )
```

```python
import functools

import jax
import jax.numpy as jnp
from jax import lax
from jax.experimental import pallas as pl
from jax.experimental.pallas import tpu as pltpu
from jax.sharding import PartitionSpec as P

SOFTEN = 0.25
LANES = 128
FORCE_ROWS = 32
EARLY = 1
LATE = 1
TABLE = 7
MESH = pl.DeviceIdType.MESH
F32 = jnp.float32
BF16 = jnp.bfloat16

QM_N, MM_Q, POT_X, POT_Z, POT_Q, GRAD_Q, GRAD_N, QMF_Z, QMF_X, MMF_Q, CODE_Q = range(11)


def split3(value):
    high = value.astype(BF16)
    rest = value - high.astype(F32)
    middle = rest.astype(BF16)
    low = (rest - middle.astype(F32)).astype(BF16)
    return high, middle, low


def kernel(
    nz,
    nq,
    nx,
    coupling,
    qm_hbm,
    species_hbm,
    count_hbm,
    owner_hbm,
    slot_hbm,
    mm_hbm,
    charge_hbm,
    table_ref,
    gain_hbm,
    message_hbm,
    hidden_hbm,
    energy_hbm,
    readout_hbm,
    atom_energy_ref,
    qm_force_ref,
    mm_force_ref,
    mm_all,
    qm_all,
    pot_x,
    pot_z,
    pot_q,
    code_q,
    grad_mine,
    grad_q,
    grad_n,
    grad_sum,
    qmf_mine,
    qmf_z,
    qmf_x,
    mmf_mine,
    mmf_q,
    wide_x,
    wide_y,
    wide_z,
    acc_x,
    acc_y,
    acc_z,
    inverses,
    cube_high,
    cube_low,
    mm_parts,
    charges,
    qm_lines,
    table_wide,
    owner_hot,
    owner_hot_t,
    slot_hot,
    qm_ref,
    species_ref,
    count_ref,
    owner_ref,
    slot_ref,
    mm_ref,
    charge_ref,
    gain_ref,
    message_ref,
    hidden_ref,
    energy_ref,
    readout_ref,
    fetch_sems,
    send_sems,
    recv_sems,
):
    blk = lax.axis_index("blk")
    rep = lax.axis_index("rep")
    z, q = blk // nq, blk % nq
    x, ring = rep // 2, (rep % 2) * nz + z
    rings = 2 * nz
    atoms = qm_ref.shape[1]
    mm_tiles = mm_ref.shape[1] // LANES
    blocks = nz * nq
    neighbours = owner_ref.shape[0]

    def at_ring(p):
        return ((p % nz) * nq + q, x * 2 + p // nz)

    def at_q(p):
        return (z * nq + p, rep)

    def shift(d):
        return (d + 1) // 2 * (2 * (d % 2) - 1)

    def zigzag(k):
        return k // 2 * (1 - 2 * (k % 2))

    def reach(d):
        return nz + zigzag(rings - d)

    def q_place(d, sign):
        y = (q // 2 + (nq // 2) + sign * (d // 2)) % (nq // 2)
        return y * 2 + (q + d) % 2

    same = lambda p: p
    near = (nz, ring, lambda d: (ring + rings - shift(d)) % rings, lambda d: (ring + rings + shift(d)) % rings, at_ring, lambda p: p % nz)
    far = (rings, ring, lambda d: (ring + reach(d)) % rings, lambda d: (ring + rings - reach(d)) % rings, at_ring, same)
    plane = (nq, q, lambda d: q_place(d, 1), lambda d: q_place(d, -1), at_q, same)
    row_x = (nx, x, lambda d: (x + d) % nx, lambda d: (x + nx - d) % nx, lambda p: (blk, p * 2 + rep % 2), same)

    def copy_to(stage, d, device, src, dst):
        return pltpu.make_async_remote_copy(
            src_ref=src,
            dst_ref=dst,
            send_sem=send_sems.at[stage, d],
            recv_sem=recv_sems.at[stage, d],
            device_id=device,
            device_id_type=MESH,
        )

    def each(axis, step):
        def body(d, carry):
            step(d)
            return carry

        lax.fori_loop(1, axis[0], body, 0)

    def outgoing(stage, axis, src_of, buffer, d):
        _, mine, to, _, device, slot = axis
        p = to(d)
        return copy_to(stage, d, device(p), src_of(p), buffer.at[slot(mine)])

    def send_all(stage, axis, src_of, buffer):
        each(axis, lambda d: outgoing(stage, axis, src_of, buffer, axis[0] - d).start())

    def sent_all(stage, axis, src_of, buffer):
        each(axis, lambda d: outgoing(stage, axis, src_of, buffer, d).wait_send())

    def wait_from(stage, axis, d, buffer):
        _, _, _, came, device, slot = axis
        p = came(d)
        place = buffer.at[slot(p)]
        copy_to(stage, d, device(p), place, place).wait_recv()
        return slot(p)

    def wait_all(stage, axis, buffer):
        def step(d):
            wait_from(stage, axis, d, buffer)

        each(axis, step)

    def total(buffer, size):
        result = buffer[0]
        for p in range(1, size):
            result = result + buffer[p]
        return result

    fetches = [
        pltpu.make_async_copy(src, dst, fetch_sems.at[k])
        for k, (src, dst) in enumerate(
            [
                (mm_hbm, mm_ref),
                (charge_hbm, charge_ref),
                (qm_hbm, qm_ref),
                (species_hbm, species_ref),
                (count_hbm, count_ref),
                (owner_hbm, owner_ref),
                (slot_hbm, slot_ref),
                (gain_hbm, gain_ref),
                (message_hbm, message_ref),
                (hidden_hbm, hidden_ref),
                (energy_hbm, energy_ref),
                (readout_hbm, readout_ref),
            ]
        )
    ]
    barrier = pltpu.get_barrier_semaphore()
    def greet(device):
        pl.semaphore_signal(barrier, inc=1, device_id=device, device_id_type=MESH)

    def greet_ring(d, carry):
        greet(at_ring((ring + d) % rings))
        greet(at_ring((ring + rings - d) % rings))
        return carry

    lax.fori_loop(1, nz // 2 + 1, greet_ring, 0)
    each(plane, lambda d: greet(at_q(plane[2](d))))
    each(row_x, lambda d: greet(row_x[4](row_x[2](d))))
    for fetch in fetches:
        fetch.start()
    for fetch in fetches[:5]:
        fetch.wait()

    mm_all[q, 0:3, :] = mm_ref[...]
    mm_all[q, 3:4, :] = charge_ref[...]
    live_row = lax.broadcasted_iota(jnp.int32, (1, atoms), 1) < count_ref[...]
    qm_all[z, 0:3, :] = qm_ref[...]
    qm_all[z, 3:4, :] = jnp.where(live_row, species_ref[...], -1).astype(F32)

    pl.semaphore_wait(barrier, nz + nq + nx - 2)
    send_all(QM_N, near, lambda p: qm_all.at[z], qm_all)
    send_all(MM_Q, plane, lambda p: mm_all.at[q], mm_all)

    for fetch in fetches[5:]:
        fetch.wait()
    table_wide[...] = jnp.zeros_like(table_wide)
    table_wide[0 : table_ref.shape[0], :] = table_ref[...].astype(F32)
    lane = lax.broadcasted_iota(jnp.int32, (atoms, LANES), 1)
    row = lax.broadcasted_iota(jnp.int32, (atoms, LANES), 0)
    for k in range(neighbours + 1):
        rows = slice(k * atoms, (k + 1) * atoms)
        if k < neighbours:
            owner = owner_ref[k : k + 1, :]
            hot_t = (row == (owner % nq) * nz + owner // nq).astype(F32)
            slots = jnp.transpose((row == slot_ref[k : k + 1, :]).astype(F32))
        else:
            hot_t = (row == q * nz + z).astype(F32)
            slots = (lane == row).astype(F32)
        owner_hot[rows, :] = jnp.transpose(hot_t).astype(BF16)
        owner_hot_t[:, rows] = hot_t[0 : owner_hot_t.shape[0], :].astype(BF16)
        slot_hot[rows, :] = slots

    def wide(line):
        return jnp.transpose(jnp.broadcast_to(line, (LANES, atoms)))

    def block_rows(p):
        return pl.ds(pl.multiple_of(p * atoms, atoms), atoms)

    def widen(p, carry):
        rows = block_rows(p)
        wide_x[rows, :] = wide(qm_all[p, 0:1, :])
        wide_y[rows, :] = wide(qm_all[p, 1:2, :])
        wide_z[rows, :] = wide(qm_all[p, 2:3, :])
        return carry

    def chunk_columns(p):
        return pl.ds(pl.multiple_of(p * mm_tiles * LANES, LANES), mm_tiles * LANES)

    def stacked(place, norm_first, order):
        norm = jnp.sum(place * place, axis=0, keepdims=True)
        one, nothing = jnp.ones_like(norm), jnp.zeros((3, norm.shape[1]), F32)
        if norm_first:
            record = jnp.concatenate([place, norm, one, nothing], axis=0)
        else:
            record = jnp.concatenate([-2.0 * place, one, norm + SOFTEN, nothing], axis=0)
        pieces = [piece.astype(F32) for piece in split3(record)]
        return jnp.concatenate([pieces[k] for k in order], axis=0)

    def take_charges(p):
        where = chunk_columns(p)
        mm_parts[:, where] = stacked(mm_all[p, 0:3, :], True, (0, 1, 0, 1, 2, 0)).astype(BF16)
        charges[:, where] = mm_all[p, 3:4, :]

    take_charges(q)
    each(plane, lambda d: take_charges(wait_from(MM_Q, plane, d, mm_all)))

    def take_block(p):
        parts = stacked(qm_all[p, 0:3, :], False, (0, 0, 1, 1, 0, 2))
        parts = jnp.concatenate([parts, jnp.zeros((LANES - 48, atoms), F32)], axis=0)
        return jnp.transpose(parts).astype(BF16)[:, 0:48]

    def potential_step(k, carry):
        @pl.when(k > 0)
        def _():
            wait_from(QM_N, near, 2 * k, qm_all)

        wait_from(QM_N, near, 2 * k + 1, qm_all)
        pair = [jnp.where(k > 0, near[5](near[3](2 * k)), z), near[5](near[3](2 * k + 1))]
        parts = jnp.concatenate([take_block(p) for p in pair], axis=0)
        square = jnp.dot(parts, mm_parts[...], preferred_element_type=F32)
        inverse = lax.rsqrt(square)
        term = inverse * charges[...]
        running = term[:, 0:LANES]
        for t in range(1, nq * mm_tiles):
            running = running + term[:, t * LANES : (t + 1) * LANES]
        for k, p in enumerate(pair):
            rows = slice(k * atoms, (k + 1) * atoms)
            inverses[block_rows(p), :] = inverse[rows, :]
            pot_x[x, pl.ds(p, 1), :] = jnp.sum(jnp.transpose(running[rows, :]), axis=0, keepdims=True)
        return carry

    lax.fori_loop(0, nz // 2, potential_step, 0)

    def columns(chunk):
        return [
            [mm_all[chunk, c : c + 1, t * LANES : (t + 1) * LANES] for c in range(4)]
            for t in range(mm_tiles)
        ]

    def lines(acc, p):
        return jnp.sum(jnp.transpose(acc[block_rows(p), :]), axis=0, keepdims=True)

    send_all(POT_X, row_x, lambda p: pot_x.at[x], pot_x)
    for p in range(nz):
        code_q[q, p : p + 1, :] = qm_all[p, 3:4, :]
    send_all(CODE_Q, plane, lambda p: code_q.at[q], code_q)
    acc_x[...] = jnp.zeros_like(acc_x)
    acc_y[...] = jnp.zeros_like(acc_y)
    acc_z[...] = jnp.zeros_like(acc_z)
    lax.fori_loop(0, nz, widen, 0)
    qm_lines[0:1, :] = jnp.ones((1, nz * atoms), F32)
    for p in range(nz):
        qm_lines[1:4, p * atoms : (p + 1) * atoms] = qm_all[p, 0:3, :]
    qm_lines[4:8, :] = jnp.zeros((4, nz * atoms), F32)

    def pull_chunk(chunk, carry):
        tiles = columns(chunk)

        def group(g, inner):
            rows = pl.ds(pl.multiple_of(g * FORCE_ROWS, FORCE_ROWS), FORCE_ROWS)
            px, py, pz = wide_x[rows, :], wide_y[rows, :], wide_z[rows, :]
            fx, fy, fz = acc_x[rows, :], acc_y[rows, :], acc_z[rows, :]
            for t, (mx, my, mz, mq) in enumerate(tiles):
                where = pl.ds(pl.multiple_of((chunk * mm_tiles + t) * LANES, LANES), LANES)
                inverse = inverses[rows, where]
                cube = inverse * inverse * inverse
                inverses[rows, where] = cube
                pull = cube * mq
                fx = fx + pull * (px - mx)
                fy = fy + pull * (py - my)
                fz = fz + pull * (pz - mz)
            acc_x[rows, :], acc_y[rows, :], acc_z[rows, :] = fx, fy, fz
            return inner

        return lax.fori_loop(0, nz * atoms // FORCE_ROWS, group, carry)

    early = min(EARLY, nq)
    lax.fori_loop(0, early, pull_chunk, 0)
    wait_all(POT_X, row_x, pot_x)
    pot_z[ring] = total(pot_x, nx)
    send_all(POT_Z, far, lambda p: pot_z.at[ring], pot_z)
    late = max(early, nq - LATE)
    lax.fori_loop(early, late, pull_chunk, 0)

    wait_all(POT_Z, far, pot_z)
    pot_q[q] = total(pot_z, rings) * coupling
    send_all(POT_Q, plane, lambda p: pot_q.at[q], pot_q)
    lax.fori_loop(late, nq, pull_chunk, 0)

    def gather_force(p, carry):
        qmf_mine[p, 0:1, :] = lines(acc_x, p)
        qmf_mine[p, 1:2, :] = lines(acc_y, p)
        qmf_mine[p, 2:3, :] = lines(acc_z, p)
        return carry

    lax.fori_loop(0, nz, gather_force, 0)
    qmf_z[ring] = qmf_mine[z]
    send_all(QMF_Z, far, lambda p: qmf_mine.at[p % nz], qmf_z)

    wait_all(CODE_Q, plane, code_q)
    codes = jnp.concatenate([code_q[p] for p in range(nq)], axis=0).astype(BF16)
    gain = gain_ref[...]
    table = table_wide[...].astype(BF16)
    bases, lives = [], []
    for k in range(neighbours + 1):
        rows = slice(k * atoms, (k + 1) * atoms)
        picked = jnp.dot(owner_hot[rows, 0:blocks], codes, preferred_element_type=F32)
        code = jnp.sum(picked * slot_hot[rows, :], axis=1, keepdims=True)
        lives.append((code >= 0).astype(F32))
        kinds = (lane.astype(F32) == code).astype(F32).astype(BF16)
        bases.append(jnp.dot(kinds, table, preferred_element_type=F32))
    wait_all(POT_Q, plane, pot_q)
    pieces = split3(jnp.concatenate([pot_q[p] for p in range(nq)], axis=0))
    neighbour = jnp.zeros((atoms, LANES), F32)
    for k in range(neighbours + 1):
        rows = slice(k * atoms, (k + 1) * atoms)
        hot = owner_hot[rows, 0:blocks]
        slots = slot_hot[rows, :]
        picked = [jnp.dot(hot, piece, preferred_element_type=F32) for piece in pieces]
        potential = jnp.sum((picked[0] + picked[1] + picked[2]) * slots, axis=1, keepdims=True)
        live = lives[k]
        start = (live * (bases[k] + potential * gain)).astype(BF16)
        if k < neighbours:
            neighbour = neighbour + start.astype(F32)
    mixed = start.astype(F32) + jnp.dot(
        neighbour.astype(BF16), message_ref[...], preferred_element_type=F32
    )
    before = jnp.dot(mixed.astype(BF16), hidden_ref[...], preferred_element_type=F32)
    sigma = jax.nn.sigmoid(before)
    active = before * sigma
    charge_part = live * jnp.sum(active * readout_ref[...], axis=1, keepdims=True)
    back_active = live * (energy_ref[...] + potential * readout_ref[...])
    back_before = (back_active * sigma * (1.0 + before * (1.0 - sigma))).astype(BF16)
    nt = (((1,), (1,)), ((), ()))
    back_mixed = lax.dot_general(back_before, hidden_ref[...], nt, preferred_element_type=F32)
    back_sum = lax.dot_general(
        back_mixed.astype(BF16), message_ref[...], nt, preferred_element_type=F32
    ).astype(BF16)
    out_going = jnp.sum(back_sum.astype(F32) * gain, axis=1, keepdims=True)
    staying = jnp.sum(back_mixed * gain, axis=1, keepdims=True) + charge_part
    spread = jnp.zeros((blocks, LANES), F32)
    parts_out, parts_stay = split3(out_going), split3(staying)
    for k in range(neighbours + 1):
        rows = slice(k * atoms, (k + 1) * atoms)
        slots = slot_hot[rows, :]
        for part in parts_out if k < neighbours else parts_stay:
            spread = spread + jnp.dot(
                owner_hot_t[0:blocks, rows],
                (slots * part.astype(F32)).astype(BF16),
                preferred_element_type=F32,
            )
    for p in range(nq):
        grad_mine[p] = spread[p * nz : (p + 1) * nz, :]
    send_all(GRAD_Q, plane, lambda p: grad_mine.at[p], grad_q)
    grad_q[q] = grad_mine[q]
    energy_part = live * jnp.sum(active * energy_ref[...], axis=1, keepdims=True)
    atom_energy = energy_part + charge_part * potential
    atom_energy_ref[...] = jnp.sum(
        jnp.where(lane == row, atom_energy, 0.0), axis=0, keepdims=True
    )

    def split_rows(g, carry):
        rows = pl.ds(pl.multiple_of(g * FORCE_ROWS, FORCE_ROWS), FORCE_ROWS)
        cube = inverses[rows, :]
        high = cube.astype(BF16)
        cube_high[rows, :] = high
        cube_low[rows, :] = (cube - high.astype(F32)).astype(BF16)
        return carry

    lax.fori_loop(0, nz * atoms // FORCE_ROWS, split_rows, 0)
    wait_all(GRAD_Q, plane, grad_q)
    grad_n[z] = total(grad_q, nq)
    send_all(GRAD_N, near, lambda p: grad_n.at[z], grad_n)
    wait_all(QMF_Z, far, qmf_z)
    qmf_x[x] = total(qmf_z, rings)
    send_all(QMF_X, row_x, lambda p: qmf_x.at[x], qmf_x)
    wait_all(GRAD_N, near, grad_n)
    live_plane = (code_q[q] >= 0).astype(F32)
    grad_sum[...] = live_plane * total(grad_n, nz)

    effective = jnp.concatenate([grad_sum[p : p + 1, :] for p in range(nz)], axis=1)
    weights = qm_lines[...] * effective
    high = weights.astype(BF16).astype(F32)
    weights = jnp.concatenate([high, weights - high], axis=0).astype(BF16)

    def push_pair(y):
        width = 2 * mm_tiles * LANES
        where = pl.ds(pl.multiple_of(y * width, width), width)
        sums = jnp.dot(weights, cube_high[:, where], preferred_element_type=F32)
        sums = sums + jnp.dot(weights, cube_low[:, where], preferred_element_type=F32)
        sums = sums[0:8, :] + sums[8:16, :]
        for c in range(2):
            part = sums[:, c * width // 2 : (c + 1) * width // 2]
            mmf_mine[2 * y + c] = part[1:4, :] - part[0:1, :] * mm_all[2 * y + c, 0:3, :]

    rows_y = nq // 2

    def push_step(k, carry):
        step = rows_y // 2 + zigzag(k)
        push_pair((q // 2 + step) % rows_y)
        for c in range(2):
            outgoing(MMF_Q, plane, lambda p: mmf_mine.at[p], mmf_q, 2 * step + c).start()
        return carry

    lax.fori_loop(1, rows_y, push_step, 0)
    push_pair(q // 2)
    outgoing(MMF_Q, plane, lambda p: mmf_mine.at[p], mmf_q, 1).start()
    mmf_q[q] = mmf_mine[q]
    sent_all(QM_N, near, lambda p: qm_all.at[z], qm_all)
    sent_all(MM_Q, plane, lambda p: mm_all.at[q], mm_all)
    sent_all(POT_X, row_x, lambda p: pot_x.at[x], pot_x)
    sent_all(POT_Z, far, lambda p: pot_z.at[ring], pot_z)
    sent_all(POT_Q, plane, lambda p: pot_q.at[q], pot_q)
    sent_all(CODE_Q, plane, lambda p: code_q.at[q], code_q)
    sent_all(QMF_Z, far, lambda p: qmf_mine.at[p % nz], qmf_z)
    sent_all(GRAD_Q, plane, lambda p: grad_mine.at[p], grad_q)
    sent_all(GRAD_N, near, lambda p: grad_n.at[z], grad_n)
    wait_all(QMF_X, row_x, qmf_x)
    qm_force_ref[...] = total(qmf_x, nx) * (grad_sum[pl.ds(z, 1), :] * coupling)
    sent_all(QMF_X, row_x, lambda p: qmf_x.at[x], qmf_x)
    sent_all(MMF_Q, plane, lambda p: mmf_mine.at[p], mmf_q)
    wait_all(MMF_Q, plane, mmf_q)
    mm_force_ref[...] = total(mmf_q, nq) * (charge_ref[...] * -coupling)


def on_device(
    nz,
    nq,
    nr,
    qm_pos,
    species,
    qm_count,
    ghost_owner,
    ghost_slot,
    mm_pos,
    mm_charge,
    species_table,
    potential_gain,
    message_weight,
    hidden_weight,
    energy_readout,
    charge_readout,
):
    atoms = qm_pos.shape[1]
    mm_here = mm_pos.shape[1]
    nx = nr // 2
    coupling = float(mm_here * nz * nq * nr) ** (-0.5)
    here = nz * atoms
    groups = ghost_owner.shape[1] + 1
    hot_rows = -(-nz * nq // 16) * 16
    arguments = (
        qm_pos,
        species[None, :],
        qm_count[None, :],
        ghost_owner.T,
        ghost_slot.T,
        mm_pos,
        mm_charge[None, :],
        species_table,
        potential_gain[None, :],
        message_weight,
        hidden_weight,
        energy_readout[None, :],
        charge_readout[None, :],
    )
    small = lambda *shape: pltpu.VMEM(shape, F32)
    vmem = pl.BlockSpec(memory_space=pltpu.VMEM)
    hbm = pl.BlockSpec(memory_space=pltpu.HBM)
    atom_energy, qm_force, mm_force = pl.pallas_call(
        functools.partial(kernel, nz, nq, nx, coupling),
        out_shape=(
            jax.ShapeDtypeStruct((1, atoms), F32),
            jax.ShapeDtypeStruct((3, atoms), F32),
            jax.ShapeDtypeStruct((3, mm_here), F32),
        ),
        in_specs=[hbm] * 7 + [vmem] + [hbm] * 5,
        out_specs=(vmem,) * 3,
        scratch_shapes=[
            small(nq, 4, mm_here),
            small(nz, 4, atoms),
            small(nx, nz, atoms),
            small(2 * nz, nz, atoms),
            small(nq, nz, atoms),
            small(nq, nz, atoms),
            small(nq, nz, atoms),
            small(nq, nz, atoms),
            small(nz, nz, atoms),
            small(nz, atoms),
            small(nz, 3, atoms),
            small(2 * nz, 3, atoms),
            small(nx, 3, atoms),
            small(nq, 3, mm_here),
            small(nq, 3, mm_here),
            *[small(here, LANES)] * 6,
            small(here, nq * mm_here),
            pltpu.VMEM((here, nq * mm_here), BF16),
            pltpu.VMEM((here, nq * mm_here), BF16),
            pltpu.VMEM((48, nq * mm_here), BF16),
            small(1, nq * mm_here),
            small(8, here),
            small(LANES, LANES),
            pltpu.VMEM((groups * atoms, LANES), BF16),
            pltpu.VMEM((hot_rows, groups * atoms), BF16),
            small(groups * atoms, LANES),
            *[pltpu.VMEM(a.shape, a.dtype) for k, a in enumerate(arguments) if k != TABLE],
            pltpu.SemaphoreType.DMA((12,)),
            pltpu.SemaphoreType.DMA((11, max(2 * nz, nq, nx))),
            pltpu.SemaphoreType.DMA((11, max(2 * nz, nq, nx))),
        ],
        compiler_params=pltpu.CompilerParams(
            collective_id=0, has_side_effects=True, vmem_limit_bytes=56 * 2**20
        ),
    )(*arguments)
    return (atom_energy[0], qm_force, mm_force)


def solution(mesh):
    blocks, nr = mesh.shape["blk"], mesh.shape["rep"]
    nq = min(8, blocks // 2)
    placed = (
        P(None, "blk"),
        P("blk"),
        P("blk"),
        P("blk", None),
        P("blk", None),
        P(None, ("blk", "rep")),
        P(("blk", "rep")),
        P(),
        P(),
        P(),
        P(),
        P(),
        P(),
    )
    return jax.shard_map(
        functools.partial(on_device, blocks // nq, nq, nr),
        mesh=mesh,
        in_specs=placed,
        out_specs=(P("blk"), P(None, "blk"), P(None, ("blk", "rep"))),
        check_vma=False,
    )
```

```python
import functools

import jax
import jax.numpy as jnp
from jax import lax
from jax.experimental import pallas as pl
from jax.experimental.pallas import tpu as pltpu
from jax.sharding import PartitionSpec as P

SOFTEN = 0.25
LANES = 128
FORCE_ROWS = 32
EARLY = 1
LATE = 1
TABLE = 7
MESH = pl.DeviceIdType.MESH
F32 = jnp.float32
BF16 = jnp.bfloat16

QM_N, MM_Q, POT_X, POT_Z, POT_Q, GRAD_Q, GRAD_N, QMF_Z, QMF_X, MMF_Q, CODE_Q = range(11)


def split3(value):
    high = value.astype(BF16)
    rest = value - high.astype(F32)
    middle = rest.astype(BF16)
    low = (rest - middle.astype(F32)).astype(BF16)
    return high, middle, low


def kernel(
    nz,
    nq,
    nx,
    coupling,
    qm_hbm,
    species_hbm,
    count_hbm,
    owner_hbm,
    slot_hbm,
    mm_hbm,
    charge_hbm,
    table_ref,
    gain_hbm,
    message_hbm,
    hidden_hbm,
    energy_hbm,
    readout_hbm,
    atom_energy_ref,
    qm_force_ref,
    mm_force_ref,
    mm_all,
    qm_all,
    pot_x,
    pot_z,
    pot_q,
    code_q,
    grad_mine,
    grad_q,
    grad_n,
    grad_sum,
    qmf_mine,
    qmf_z,
    qmf_x,
    mmf_mine,
    mmf_q,
    wide_x,
    wide_y,
    wide_z,
    acc_x,
    acc_y,
    acc_z,
    inverses,
    cube_high,
    cube_low,
    mm_parts,
    charges,
    qm_lines,
    table_wide,
    owner_hot,
    owner_hot_t,
    slot_hot,
    qm_ref,
    species_ref,
    count_ref,
    owner_ref,
    slot_ref,
    mm_ref,
    charge_ref,
    gain_ref,
    message_ref,
    hidden_ref,
    energy_ref,
    readout_ref,
    fetch_sems,
    send_sems,
    recv_sems,
):
    blk = lax.axis_index("blk")
    rep = lax.axis_index("rep")
    z, q = blk // nq, blk % nq
    x, ring = rep // 2, (rep % 2) * nz + z
    rings = 2 * nz
    atoms = qm_ref.shape[1]
    mm_tiles = mm_ref.shape[1] // LANES
    blocks = nz * nq
    neighbours = owner_ref.shape[0]

    def at_ring(p):
        return ((p % nz) * nq + q, x * 2 + p // nz)

    def at_q(p):
        return (z * nq + p, rep)

    def shift(d):
        return (d + 1) // 2 * (2 * (d % 2) - 1)

    def zigzag(k):
        return k // 2 * (1 - 2 * (k % 2))

    def reach(d):
        return nz + zigzag(rings - d)

    def q_place(d, sign):
        y = (q // 2 + (nq // 2) + sign * (d // 2)) % (nq // 2)
        return y * 2 + (q + d) % 2

    same = lambda p: p
    near = (nz, ring, lambda d: (ring + rings - shift(d)) % rings, lambda d: (ring + rings + shift(d)) % rings, at_ring, lambda p: p % nz)
    far = (rings, ring, lambda d: (ring + reach(d)) % rings, lambda d: (ring + rings - reach(d)) % rings, at_ring, same)
    plane = (nq, q, lambda d: q_place(d, 1), lambda d: q_place(d, -1), at_q, same)
    row_x = (nx, x, lambda d: (x + d) % nx, lambda d: (x + nx - d) % nx, lambda p: (blk, p * 2 + rep % 2), same)

    def copy_to(stage, d, device, src, dst):
        return pltpu.make_async_remote_copy(
            src_ref=src,
            dst_ref=dst,
            send_sem=send_sems.at[stage, d],
            recv_sem=recv_sems.at[stage, d],
            device_id=device,
            device_id_type=MESH,
        )

    def each(axis, step):
        def body(d, carry):
            step(d)
            return carry

        lax.fori_loop(1, axis[0], body, 0)

    def outgoing(stage, axis, src_of, buffer, d):
        _, mine, to, _, device, slot = axis
        p = to(d)
        return copy_to(stage, d, device(p), src_of(p), buffer.at[slot(mine)])

    def send_all(stage, axis, src_of, buffer):
        each(axis, lambda d: outgoing(stage, axis, src_of, buffer, axis[0] - d).start())

    def sent_all(stage, axis, src_of, buffer):
        each(axis, lambda d: outgoing(stage, axis, src_of, buffer, d).wait_send())

    def wait_from(stage, axis, d, buffer):
        _, _, _, came, device, slot = axis
        p = came(d)
        place = buffer.at[slot(p)]
        copy_to(stage, d, device(p), place, place).wait_recv()
        return slot(p)

    def wait_all(stage, axis, buffer):
        def step(d):
            wait_from(stage, axis, d, buffer)

        each(axis, step)

    def total(buffer, size):
        result = buffer[0]
        for p in range(1, size):
            result = result + buffer[p]
        return result

    fetches = [
        pltpu.make_async_copy(src, dst, fetch_sems.at[k])
        for k, (src, dst) in enumerate(
            [
                (mm_hbm, mm_ref),
                (charge_hbm, charge_ref),
                (qm_hbm, qm_ref),
                (species_hbm, species_ref),
                (count_hbm, count_ref),
                (owner_hbm, owner_ref),
                (slot_hbm, slot_ref),
                (gain_hbm, gain_ref),
                (message_hbm, message_ref),
                (hidden_hbm, hidden_ref),
                (energy_hbm, energy_ref),
                (readout_hbm, readout_ref),
            ]
        )
    ]
    barrier = pltpu.get_barrier_semaphore()
    def greet(device):
        pl.semaphore_signal(barrier, inc=1, device_id=device, device_id_type=MESH)

    def greet_ring(d, carry):
        greet(at_ring((ring + d) % rings))
        greet(at_ring((ring + rings - d) % rings))
        return carry

    lax.fori_loop(1, nz // 2 + 1, greet_ring, 0)
    each(plane, lambda d: greet(at_q(plane[2](d))))
    each(row_x, lambda d: greet(row_x[4](row_x[2](d))))
    for fetch in fetches:
        fetch.start()
    for fetch in fetches[:5]:
        fetch.wait()

    mm_all[q, 0:3, :] = mm_ref[...]
    mm_all[q, 3:4, :] = charge_ref[...]
    live_row = lax.broadcasted_iota(jnp.int32, (1, atoms), 1) < count_ref[...]
    qm_all[z, 0:3, :] = qm_ref[...]
    qm_all[z, 3:4, :] = jnp.where(live_row, species_ref[...], -1).astype(F32)

    pl.semaphore_wait(barrier, nz + nq + nx - 2)
    send_all(QM_N, near, lambda p: qm_all.at[z], qm_all)
    send_all(MM_Q, plane, lambda p: mm_all.at[q], mm_all)

    for fetch in fetches[5:]:
        fetch.wait()
    table_wide[...] = jnp.zeros_like(table_wide)
    table_wide[0 : table_ref.shape[0], :] = table_ref[...].astype(F32)
    lane = lax.broadcasted_iota(jnp.int32, (atoms, LANES), 1)
    row = lax.broadcasted_iota(jnp.int32, (atoms, LANES), 0)
    for k in range(neighbours + 1):
        rows = slice(k * atoms, (k + 1) * atoms)
        if k < neighbours:
            owner = owner_ref[k : k + 1, :]
            hot_t = (row == (owner % nq) * nz + owner // nq).astype(F32)
            slots = jnp.transpose((row == slot_ref[k : k + 1, :]).astype(F32))
        else:
            hot_t = (row == q * nz + z).astype(F32)
            slots = (lane == row).astype(F32)
        owner_hot[rows, :] = jnp.transpose(hot_t).astype(BF16)
        owner_hot_t[:, rows] = hot_t[0 : owner_hot_t.shape[0], :].astype(BF16)
        slot_hot[rows, :] = slots

    def wide(line):
        return jnp.transpose(jnp.broadcast_to(line, (LANES, atoms)))

    def block_rows(p):
        return pl.ds(pl.multiple_of(p * atoms, atoms), atoms)

    def widen(p, carry):
        rows = block_rows(p)
        wide_x[rows, :] = wide(qm_all[p, 0:1, :])
        wide_y[rows, :] = wide(qm_all[p, 1:2, :])
        wide_z[rows, :] = wide(qm_all[p, 2:3, :])
        return carry

    def chunk_columns(p):
        return pl.ds(pl.multiple_of(p * mm_tiles * LANES, LANES), mm_tiles * LANES)

    def stacked(place, norm_first, order):
        norm = jnp.sum(place * place, axis=0, keepdims=True)
        one, nothing = jnp.ones_like(norm), jnp.zeros((3, norm.shape[1]), F32)
        if norm_first:
            record = jnp.concatenate([place, norm, one, nothing], axis=0)
        else:
            record = jnp.concatenate([-2.0 * place, one, norm + SOFTEN, nothing], axis=0)
        pieces = [piece.astype(F32) for piece in split3(record)]
        return jnp.concatenate([pieces[k] for k in order], axis=0)

    def take_charges(p):
        where = chunk_columns(p)
        mm_parts[:, where] = stacked(mm_all[p, 0:3, :], True, (0, 1, 0, 1, 2, 0)).astype(BF16)
        charges[:, where] = mm_all[p, 3:4, :]

    take_charges(q)
    each(plane, lambda d: take_charges(wait_from(MM_Q, plane, d, mm_all)))

    def take_block(p):
        parts = stacked(qm_all[p, 0:3, :], False, (0, 0, 1, 1, 0, 2))
        parts = jnp.concatenate([parts, jnp.zeros((LANES - 48, atoms), F32)], axis=0)
        return jnp.transpose(parts).astype(BF16)[:, 0:48]

    def potential_step(k, carry):
        @pl.when(k > 0)
        def _():
            wait_from(QM_N, near, 2 * k, qm_all)

        wait_from(QM_N, near, 2 * k + 1, qm_all)
        pair = [jnp.where(k > 0, near[5](near[3](2 * k)), z), near[5](near[3](2 * k + 1))]
        parts = jnp.concatenate([take_block(p) for p in pair], axis=0)
        square = jnp.dot(parts, mm_parts[...], preferred_element_type=F32)
        inverse = lax.rsqrt(square)
        term = inverse * charges[...]
        running = term[:, 0:LANES]
        for t in range(1, nq * mm_tiles):
            running = running + term[:, t * LANES : (t + 1) * LANES]
        for k, p in enumerate(pair):
            rows = slice(k * atoms, (k + 1) * atoms)
            inverses[block_rows(p), :] = inverse[rows, :]
            pot_x[x, pl.ds(p, 1), :] = jnp.sum(jnp.transpose(running[rows, :]), axis=0, keepdims=True)
        return carry

    lax.fori_loop(0, nz // 2, potential_step, 0)

    def columns(chunk):
        return [
            [mm_all[chunk, c : c + 1, t * LANES : (t + 1) * LANES] for c in range(4)]
            for t in range(mm_tiles)
        ]

    def lines(acc, p):
        return jnp.sum(jnp.transpose(acc[block_rows(p), :]), axis=0, keepdims=True)

    send_all(POT_X, row_x, lambda p: pot_x.at[x], pot_x)
    for p in range(nz):
        code_q[q, p : p + 1, :] = qm_all[p, 3:4, :]
    send_all(CODE_Q, plane, lambda p: code_q.at[q], code_q)
    acc_x[...] = jnp.zeros_like(acc_x)
    acc_y[...] = jnp.zeros_like(acc_y)
    acc_z[...] = jnp.zeros_like(acc_z)
    lax.fori_loop(0, nz, widen, 0)
    qm_lines[0:1, :] = jnp.ones((1, nz * atoms), F32)
    for p in range(nz):
        qm_lines[1:4, p * atoms : (p + 1) * atoms] = qm_all[p, 0:3, :]
    qm_lines[4:8, :] = jnp.zeros((4, nz * atoms), F32)

    def pull_chunk(chunk, carry):
        tiles = columns(chunk)

        def group(g, inner):
            rows = pl.ds(pl.multiple_of(g * FORCE_ROWS, FORCE_ROWS), FORCE_ROWS)
            px, py, pz = wide_x[rows, :], wide_y[rows, :], wide_z[rows, :]
            fx, fy, fz = acc_x[rows, :], acc_y[rows, :], acc_z[rows, :]
            for t, (mx, my, mz, mq) in enumerate(tiles):
                where = pl.ds(pl.multiple_of((chunk * mm_tiles + t) * LANES, LANES), LANES)
                inverse = inverses[rows, where]
                cube = inverse * inverse * inverse
                inverses[rows, where] = cube
                pull = cube * mq
                fx = fx + pull * (px - mx)
                fy = fy + pull * (py - my)
                fz = fz + pull * (pz - mz)
            acc_x[rows, :], acc_y[rows, :], acc_z[rows, :] = fx, fy, fz
            return inner

        return lax.fori_loop(0, nz * atoms // FORCE_ROWS, group, carry)

    early = min(EARLY, nq)
    lax.fori_loop(0, early, pull_chunk, 0)
    wait_all(POT_X, row_x, pot_x)
    pot_z[ring] = total(pot_x, nx)
    send_all(POT_Z, far, lambda p: pot_z.at[ring], pot_z)
    late = max(early, nq - LATE)
    lax.fori_loop(early, late, pull_chunk, 0)

    wait_all(POT_Z, far, pot_z)
    pot_q[q] = total(pot_z, rings) * coupling
    send_all(POT_Q, plane, lambda p: pot_q.at[q], pot_q)
    lax.fori_loop(late, nq, pull_chunk, 0)

    def gather_force(p, carry):
        qmf_mine[p, 0:1, :] = lines(acc_x, p)
        qmf_mine[p, 1:2, :] = lines(acc_y, p)
        qmf_mine[p, 2:3, :] = lines(acc_z, p)
        return carry

    lax.fori_loop(0, nz, gather_force, 0)
    qmf_z[ring] = qmf_mine[z]
    send_all(QMF_Z, far, lambda p: qmf_mine.at[p % nz], qmf_z)

    wait_all(CODE_Q, plane, code_q)
    codes = jnp.concatenate([code_q[p] for p in range(nq)], axis=0).astype(BF16)
    gain = gain_ref[...]
    table = table_wide[...].astype(BF16)
    bases, lives = [], []
    for k in range(neighbours + 1):
        rows = slice(k * atoms, (k + 1) * atoms)
        picked = jnp.dot(owner_hot[rows, 0:blocks], codes, preferred_element_type=F32)
        code = jnp.sum(picked * slot_hot[rows, :], axis=1, keepdims=True)
        lives.append((code >= 0).astype(F32))
        kinds = (lane.astype(F32) == code).astype(F32).astype(BF16)
        bases.append(jnp.dot(kinds, table, preferred_element_type=F32))
    wait_all(POT_Q, plane, pot_q)
    pieces = split3(jnp.concatenate([pot_q[p] for p in range(nq)], axis=0))
    neighbour = jnp.zeros((atoms, LANES), F32)
    for k in range(neighbours + 1):
        rows = slice(k * atoms, (k + 1) * atoms)
        hot = owner_hot[rows, 0:blocks]
        slots = slot_hot[rows, :]
        picked = [jnp.dot(hot, piece, preferred_element_type=F32) for piece in pieces]
        potential = jnp.sum((picked[0] + picked[1] + picked[2]) * slots, axis=1, keepdims=True)
        live = lives[k]
        start = (live * (bases[k] + potential * gain)).astype(BF16)
        if k < neighbours:
            neighbour = neighbour + start.astype(F32)
    mixed = start.astype(F32) + jnp.dot(
        neighbour.astype(BF16), message_ref[...], preferred_element_type=F32
    )
    before = jnp.dot(mixed.astype(BF16), hidden_ref[...], preferred_element_type=F32)
    sigma = jax.nn.sigmoid(before)
    active = before * sigma
    charge_part = live * jnp.sum(active * readout_ref[...], axis=1, keepdims=True)
    back_active = live * (energy_ref[...] + potential * readout_ref[...])
    back_before = (back_active * sigma * (1.0 + before * (1.0 - sigma))).astype(BF16)
    nt = (((1,), (1,)), ((), ()))
    back_mixed = lax.dot_general(back_before, hidden_ref[...], nt, preferred_element_type=F32)
    back_sum = lax.dot_general(
        back_mixed.astype(BF16), message_ref[...], nt, preferred_element_type=F32
    ).astype(BF16)
    out_going = jnp.sum(back_sum.astype(F32) * gain, axis=1, keepdims=True)
    staying = jnp.sum(back_mixed * gain, axis=1, keepdims=True) + charge_part
    spread = jnp.zeros((blocks, LANES), F32)
    parts_out, parts_stay = split3(out_going), split3(staying)
    for k in range(neighbours + 1):
        rows = slice(k * atoms, (k + 1) * atoms)
        slots = slot_hot[rows, :]
        for part in parts_out if k < neighbours else parts_stay:
            spread = spread + jnp.dot(
                owner_hot_t[0:blocks, rows],
                (slots * part.astype(F32)).astype(BF16),
                preferred_element_type=F32,
            )
    for p in range(nq):
        grad_mine[p] = spread[p * nz : (p + 1) * nz, :]
    send_all(GRAD_Q, plane, lambda p: grad_mine.at[p], grad_q)
    grad_q[q] = grad_mine[q]
    energy_part = live * jnp.sum(active * energy_ref[...], axis=1, keepdims=True)
    atom_energy = energy_part + charge_part * potential
    atom_energy_ref[...] = jnp.sum(
        jnp.where(lane == row, atom_energy, 0.0), axis=0, keepdims=True
    )

    def split_rows(g, carry):
        rows = pl.ds(pl.multiple_of(g * FORCE_ROWS, FORCE_ROWS), FORCE_ROWS)
        cube = inverses[rows, :]
        high = cube.astype(BF16)
        cube_high[rows, :] = high
        cube_low[rows, :] = (cube - high.astype(F32)).astype(BF16)
        return carry

    lax.fori_loop(0, nz * atoms // FORCE_ROWS, split_rows, 0)
    wait_all(GRAD_Q, plane, grad_q)
    grad_n[z] = total(grad_q, nq)
    send_all(GRAD_N, near, lambda p: grad_n.at[z], grad_n)
    wait_all(QMF_Z, far, qmf_z)
    qmf_x[x] = total(qmf_z, rings)
    send_all(QMF_X, row_x, lambda p: qmf_x.at[x], qmf_x)
    wait_all(GRAD_N, near, grad_n)
    live_plane = (code_q[q] >= 0).astype(F32)
    grad_sum[...] = live_plane * total(grad_n, nz)

    effective = jnp.concatenate([grad_sum[p : p + 1, :] for p in range(nz)], axis=1)
    weights = qm_lines[...] * effective
    high = weights.astype(BF16).astype(F32)
    weights = jnp.concatenate([high, weights - high], axis=0).astype(BF16)

    def push_pair(y):
        width = 2 * mm_tiles * LANES
        where = pl.ds(pl.multiple_of(y * width, width), width)
        sums = jnp.dot(weights, cube_high[:, where], preferred_element_type=F32)
        sums = sums + jnp.dot(weights, cube_low[:, where], preferred_element_type=F32)
        sums = sums[0:8, :] + sums[8:16, :]
        for c in range(2):
            part = sums[:, c * width // 2 : (c + 1) * width // 2]
            mmf_mine[2 * y + c] = part[1:4, :] - part[0:1, :] * mm_all[2 * y + c, 0:3, :]

    rows_y = nq // 2

    def push_step(k, carry):
        step = rows_y // 2 + zigzag(k)
        push_pair((q // 2 + step) % rows_y)
        for c in range(2):
            outgoing(MMF_Q, plane, lambda p: mmf_mine.at[p], mmf_q, 2 * step + c).start()
        return carry

    lax.fori_loop(1, rows_y, push_step, 0)
    push_pair(q // 2)
    outgoing(MMF_Q, plane, lambda p: mmf_mine.at[p], mmf_q, 1).start()
    mmf_q[q] = mmf_mine[q]
    sent_all(QM_N, near, lambda p: qm_all.at[z], qm_all)
    sent_all(MM_Q, plane, lambda p: mm_all.at[q], mm_all)
    sent_all(POT_X, row_x, lambda p: pot_x.at[x], pot_x)
    sent_all(POT_Z, far, lambda p: pot_z.at[ring], pot_z)
    sent_all(POT_Q, plane, lambda p: pot_q.at[q], pot_q)
    sent_all(CODE_Q, plane, lambda p: code_q.at[q], code_q)
    sent_all(QMF_Z, far, lambda p: qmf_mine.at[p % nz], qmf_z)
    sent_all(GRAD_Q, plane, lambda p: grad_mine.at[p], grad_q)
    sent_all(GRAD_N, near, lambda p: grad_n.at[z], grad_n)
    wait_all(QMF_X, row_x, qmf_x)
    qm_force_ref[...] = total(qmf_x, nx) * (grad_sum[pl.ds(z, 1), :] * coupling)
    sent_all(QMF_X, row_x, lambda p: qmf_x.at[x], qmf_x)
    sent_all(MMF_Q, plane, lambda p: mmf_mine.at[p], mmf_q)
    wait_all(MMF_Q, plane, mmf_q)
    mm_force_ref[...] = total(mmf_q, nq) * (charge_ref[...] * -coupling)


def on_device(
    nz,
    nq,
    nr,
    qm_pos,
    species,
    qm_count,
    ghost_owner,
    ghost_slot,
    mm_pos,
    mm_charge,
    species_table,
    potential_gain,
    message_weight,
    hidden_weight,
    energy_readout,
    charge_readout,
):
    atoms = qm_pos.shape[1]
    mm_here = mm_pos.shape[1]
    nx = nr // 2
    coupling = float(mm_here * nz * nq * nr) ** (-0.5)
    here = nz * atoms
    groups = ghost_owner.shape[1] + 1
    hot_rows = -(-nz * nq // 16) * 16
    arguments = (
        qm_pos,
        species[None, :],
        qm_count[None, :],
        ghost_owner.T,
        ghost_slot.T,
        mm_pos,
        mm_charge[None, :],
        species_table,
        potential_gain[None, :],
        message_weight,
        hidden_weight,
        energy_readout[None, :],
        charge_readout[None, :],
    )
    small = lambda *shape: pltpu.VMEM(shape, F32)
    vmem = pl.BlockSpec(memory_space=pltpu.VMEM)
    hbm = pl.BlockSpec(memory_space=pltpu.HBM)
    atom_energy, qm_force, mm_force = pl.pallas_call(
        functools.partial(kernel, nz, nq, nx, coupling),
        out_shape=(
            jax.ShapeDtypeStruct((1, atoms), F32),
            jax.ShapeDtypeStruct((3, atoms), F32),
            jax.ShapeDtypeStruct((3, mm_here), F32),
        ),
        in_specs=[hbm] * 7 + [vmem] + [hbm] * 5,
        out_specs=(vmem,) * 3,
        scratch_shapes=[
            small(nq, 4, mm_here),
            small(nz, 4, atoms),
            small(nx, nz, atoms),
            small(2 * nz, nz, atoms),
            small(nq, nz, atoms),
            small(nq, nz, atoms),
            small(nq, nz, atoms),
            small(nq, nz, atoms),
            small(nz, nz, atoms),
            small(nz, atoms),
            small(nz, 3, atoms),
            small(2 * nz, 3, atoms),
            small(nx, 3, atoms),
            small(nq, 3, mm_here),
            small(nq, 3, mm_here),
            *[small(here, LANES)] * 6,
            small(here, nq * mm_here),
            pltpu.VMEM((here, nq * mm_here), BF16),
            pltpu.VMEM((here, nq * mm_here), BF16),
            pltpu.VMEM((48, nq * mm_here), BF16),
            small(1, nq * mm_here),
            small(8, here),
            small(LANES, LANES),
            pltpu.VMEM((groups * atoms, LANES), BF16),
            pltpu.VMEM((hot_rows, groups * atoms), BF16),
            small(groups * atoms, LANES),
            *[pltpu.VMEM(a.shape, a.dtype) for k, a in enumerate(arguments) if k != TABLE],
            pltpu.SemaphoreType.DMA((12,)),
            pltpu.SemaphoreType.DMA((11, max(2 * nz, nq, nx))),
            pltpu.SemaphoreType.DMA((11, max(2 * nz, nq, nx))),
        ],
        compiler_params=pltpu.CompilerParams(
            collective_id=0, has_side_effects=True, vmem_limit_bytes=55176 * 2**10
        ),
    )(*arguments)
    return (atom_energy[0], qm_force, mm_force)


def solution(mesh):
    blocks, nr = mesh.shape["blk"], mesh.shape["rep"]
    nq = min(8, blocks // 2)
    placed = (
        P(None, "blk"),
        P("blk"),
        P("blk"),
        P("blk", None),
        P("blk", None),
        P(None, ("blk", "rep")),
        P(("blk", "rep")),
        P(),
        P(),
        P(),
        P(),
        P(),
        P(),
    )
    return jax.shard_map(
        functools.partial(on_device, blocks // nq, nq, nr),
        mesh=mesh,
        in_specs=placed,
        out_specs=(P("blk"), P(None, "blk"), P(None, ("blk", "rep"))),
        check_vma=False,
    )
```

```python
import functools

import jax
import jax.numpy as jnp
from jax import lax
from jax.experimental import pallas as pl
from jax.experimental.pallas import tpu as pltpu
from jax.sharding import PartitionSpec as P

SOFTEN = 0.25
LANES = 128
FORCE_ROWS = 32
EARLY = 1
LATE = 1
TABLE = 7
MESH = pl.DeviceIdType.MESH
F32 = jnp.float32
BF16 = jnp.bfloat16

QM_N, MM_Q, POT_X, POT_Z, POT_Q, GRAD_Q, GRAD_N, QMF_Z, QMF_X, MMF_Q, CODE_Q = range(11)


def split3(value):
    high = value.astype(BF16)
    rest = value - high.astype(F32)
    middle = rest.astype(BF16)
    low = (rest - middle.astype(F32)).astype(BF16)
    return high, middle, low


def kernel(
    nz,
    nq,
    nx,
    coupling,
    qm_hbm,
    species_hbm,
    count_hbm,
    owner_hbm,
    slot_hbm,
    mm_hbm,
    charge_hbm,
    table_ref,
    gain_hbm,
    message_hbm,
    hidden_hbm,
    energy_hbm,
    readout_hbm,
    atom_energy_ref,
    qm_force_ref,
    mm_force_ref,
    mm_all,
    qm_all,
    pot_x,
    pot_z,
    pot_q,
    code_q,
    grad_mine,
    grad_q,
    grad_n,
    grad_sum,
    qmf_mine,
    qmf_z,
    qmf_x,
    mmf_mine,
    mmf_q,
    wide_x,
    wide_y,
    wide_z,
    acc_x,
    acc_y,
    acc_z,
    inverses,
    cube_high,
    cube_low,
    mm_parts,
    charges,
    qm_lines,
    table_wide,
    owner_hot,
    owner_hot_t,
    slot_hot,
    qm_ref,
    species_ref,
    count_ref,
    owner_ref,
    slot_ref,
    mm_ref,
    charge_ref,
    gain_ref,
    message_ref,
    hidden_ref,
    energy_ref,
    readout_ref,
    fetch_sems,
    send_sems,
    recv_sems,
):
    blk = lax.axis_index("blk")
    rep = lax.axis_index("rep")
    z, q = blk // nq, blk % nq
    x, ring = rep // 2, (rep % 2) * nz + z
    rings = 2 * nz
    atoms = qm_ref.shape[1]
    mm_tiles = mm_ref.shape[1] // LANES
    blocks = nz * nq
    neighbours = owner_ref.shape[0]

    def at_ring(p):
        return ((p % nz) * nq + q, x * 2 + p // nz)

    def at_q(p):
        return (z * nq + p, rep)

    def shift(d):
        return (d + 1) // 2 * (2 * (d % 2) - 1)

    def zigzag(k):
        return k // 2 * (1 - 2 * (k % 2))

    def reach(d):
        return nz + zigzag(rings - d)

    def q_place(d, sign):
        y = (q // 2 + (nq // 2) + sign * (d // 2)) % (nq // 2)
        return y * 2 + (q + d) % 2

    same = lambda p: p
    near = (nz, ring, lambda d: (ring + rings - shift(d)) % rings, lambda d: (ring + rings + shift(d)) % rings, at_ring, lambda p: p % nz)
    far = (rings, ring, lambda d: (ring + reach(d)) % rings, lambda d: (ring + rings - reach(d)) % rings, at_ring, same)
    plane = (nq, q, lambda d: q_place(d, 1), lambda d: q_place(d, -1), at_q, same)
    row_x = (nx, x, lambda d: (x + d) % nx, lambda d: (x + nx - d) % nx, lambda p: (blk, p * 2 + rep % 2), same)

    def copy_to(stage, d, device, src, dst):
        return pltpu.make_async_remote_copy(
            src_ref=src,
            dst_ref=dst,
            send_sem=send_sems.at[stage, d],
            recv_sem=recv_sems.at[stage, d],
            device_id=device,
            device_id_type=MESH,
        )

    def each(axis, step):
        def body(d, carry):
            step(d)
            return carry

        lax.fori_loop(1, axis[0], body, 0)

    def outgoing(stage, axis, src_of, buffer, d):
        _, mine, to, _, device, slot = axis
        p = to(d)
        return copy_to(stage, d, device(p), src_of(p), buffer.at[slot(mine)])

    def send_all(stage, axis, src_of, buffer):
        each(axis, lambda d: outgoing(stage, axis, src_of, buffer, axis[0] - d).start())

    def sent_all(stage, axis, src_of, buffer):
        each(axis, lambda d: outgoing(stage, axis, src_of, buffer, d).wait_send())

    def wait_from(stage, axis, d, buffer):
        _, _, _, came, device, slot = axis
        p = came(d)
        place = buffer.at[slot(p)]
        copy_to(stage, d, device(p), place, place).wait_recv()
        return slot(p)

    def wait_all(stage, axis, buffer):
        def step(d):
            wait_from(stage, axis, d, buffer)

        each(axis, step)

    def total(buffer, size):
        result = buffer[0]
        for p in range(1, size):
            result = result + buffer[p]
        return result

    fetches = [
        pltpu.make_async_copy(src, dst, fetch_sems.at[k])
        for k, (src, dst) in enumerate(
            [
                (mm_hbm, mm_ref),
                (charge_hbm, charge_ref),
                (qm_hbm, qm_ref),
                (species_hbm, species_ref),
                (count_hbm, count_ref),
                (owner_hbm, owner_ref),
                (slot_hbm, slot_ref),
                (gain_hbm, gain_ref),
                (message_hbm, message_ref),
                (hidden_hbm, hidden_ref),
                (energy_hbm, energy_ref),
                (readout_hbm, readout_ref),
            ]
        )
    ]
    barrier = pltpu.get_barrier_semaphore()
    def greet(device):
        pl.semaphore_signal(barrier, inc=1, device_id=device, device_id_type=MESH)

    def greet_ring(d, carry):
        greet(at_ring((ring + d) % rings))
        greet(at_ring((ring + rings - d) % rings))
        return carry

    lax.fori_loop(1, nz // 2 + 1, greet_ring, 0)
    each(plane, lambda d: greet(at_q(plane[2](d))))
    each(row_x, lambda d: greet(row_x[4](row_x[2](d))))
    for fetch in fetches:
        fetch.start()
    for fetch in fetches[:5]:
        fetch.wait()

    mm_all[q, 0:3, :] = mm_ref[...]
    mm_all[q, 3:4, :] = charge_ref[...]
    live_row = lax.broadcasted_iota(jnp.int32, (1, atoms), 1) < count_ref[...]
    qm_all[z, 0:3, :] = qm_ref[...]
    qm_all[z, 3:4, :] = jnp.where(live_row, species_ref[...], -1).astype(F32)

    pl.semaphore_wait(barrier, nz + nq + nx - 2)
    send_all(QM_N, near, lambda p: qm_all.at[z], qm_all)
    send_all(MM_Q, plane, lambda p: mm_all.at[q], mm_all)

    for fetch in fetches[5:]:
        fetch.wait()
    table_wide[...] = jnp.zeros_like(table_wide)
    table_wide[0 : table_ref.shape[0], :] = table_ref[...].astype(F32)
    lane = lax.broadcasted_iota(jnp.int32, (atoms, LANES), 1)
    row = lax.broadcasted_iota(jnp.int32, (atoms, LANES), 0)
    for k in range(neighbours + 1):
        rows = slice(k * atoms, (k + 1) * atoms)
        if k < neighbours:
            owner = owner_ref[k : k + 1, :]
            hot_t = (row == (owner % nq) * nz + owner // nq).astype(F32)
            slots = jnp.transpose((row == slot_ref[k : k + 1, :]).astype(F32))
        else:
            hot_t = (row == q * nz + z).astype(F32)
            slots = (lane == row).astype(F32)
        owner_hot[rows, :] = jnp.transpose(hot_t).astype(BF16)
        owner_hot_t[:, rows] = hot_t[0 : owner_hot_t.shape[0], :].astype(BF16)
        slot_hot[rows, :] = slots

    def wide(line):
        return jnp.transpose(jnp.broadcast_to(line, (LANES, atoms)))

    def block_rows(p):
        return pl.ds(pl.multiple_of(p * atoms, atoms), atoms)

    def widen(p, carry):
        rows = block_rows(p)
        wide_x[rows, :] = wide(qm_all[p, 0:1, :])
        wide_y[rows, :] = wide(qm_all[p, 1:2, :])
        wide_z[rows, :] = wide(qm_all[p, 2:3, :])
        return carry

    def chunk_columns(p):
        return pl.ds(pl.multiple_of(p * mm_tiles * LANES, LANES), mm_tiles * LANES)

    def stacked(place, norm_first, order):
        norm = jnp.sum(place * place, axis=0, keepdims=True)
        one, nothing = jnp.ones_like(norm), jnp.zeros((3, norm.shape[1]), F32)
        if norm_first:
            record = jnp.concatenate([place, norm, one, nothing], axis=0)
        else:
            record = jnp.concatenate([-2.0 * place, one, norm + SOFTEN, nothing], axis=0)
        pieces = [piece.astype(F32) for piece in split3(record)]
        return jnp.concatenate([pieces[k] for k in order], axis=0)

    def take_charges(p):
        where = chunk_columns(p)
        mm_parts[:, where] = stacked(mm_all[p, 0:3, :], True, (0, 1, 0, 1, 2, 0)).astype(BF16)
        charges[:, where] = mm_all[p, 3:4, :]

    take_charges(q)
    each(plane, lambda d: take_charges(wait_from(MM_Q, plane, d, mm_all)))

    def take_block(p):
        parts = stacked(qm_all[p, 0:3, :], False, (0, 0, 1, 1, 0, 2))
        parts = jnp.concatenate([parts, jnp.zeros((LANES - 48, atoms), F32)], axis=0)
        return jnp.transpose(parts).astype(BF16)[:, 0:48]

    def potential_step(k, carry):
        @pl.when(k > 0)
        def _():
            wait_from(QM_N, near, 2 * k, qm_all)

        wait_from(QM_N, near, 2 * k + 1, qm_all)
        pair = [jnp.where(k > 0, near[5](near[3](2 * k)), z), near[5](near[3](2 * k + 1))]
        parts = jnp.concatenate([take_block(p) for p in pair], axis=0)
        square = jnp.dot(parts, mm_parts[...], preferred_element_type=F32)
        inverse = lax.rsqrt(square)
        term = inverse * charges[...]
        running = term[:, 0:LANES]
        for t in range(1, nq * mm_tiles):
            running = running + term[:, t * LANES : (t + 1) * LANES]
        for k, p in enumerate(pair):
            rows = slice(k * atoms, (k + 1) * atoms)
            inverses[block_rows(p), :] = inverse[rows, :]
            pot_x[x, pl.ds(p, 1), :] = jnp.sum(jnp.transpose(running[rows, :]), axis=0, keepdims=True)
        return carry

    for k in range(nz // 2):
        potential_step(k, 0)

    def columns(chunk):
        return [
            [mm_all[chunk, c : c + 1, t * LANES : (t + 1) * LANES] for c in range(4)]
            for t in range(mm_tiles)
        ]

    def lines(acc, p):
        return jnp.sum(jnp.transpose(acc[block_rows(p), :]), axis=0, keepdims=True)

    send_all(POT_X, row_x, lambda p: pot_x.at[x], pot_x)
    for p in range(nz):
        code_q[q, p : p + 1, :] = qm_all[p, 3:4, :]
    send_all(CODE_Q, plane, lambda p: code_q.at[q], code_q)
    acc_x[...] = jnp.zeros_like(acc_x)
    acc_y[...] = jnp.zeros_like(acc_y)
    acc_z[...] = jnp.zeros_like(acc_z)
    lax.fori_loop(0, nz, widen, 0)
    qm_lines[0:1, :] = jnp.ones((1, nz * atoms), F32)
    for p in range(nz):
        qm_lines[1:4, p * atoms : (p + 1) * atoms] = qm_all[p, 0:3, :]
    qm_lines[4:8, :] = jnp.zeros((4, nz * atoms), F32)

    def pull_chunk(chunk, carry):
        tiles = columns(chunk)

        def group(g, inner):
            rows = pl.ds(pl.multiple_of(g * FORCE_ROWS, FORCE_ROWS), FORCE_ROWS)
            px, py, pz = wide_x[rows, :], wide_y[rows, :], wide_z[rows, :]
            fx, fy, fz = acc_x[rows, :], acc_y[rows, :], acc_z[rows, :]
            for t, (mx, my, mz, mq) in enumerate(tiles):
                where = pl.ds(pl.multiple_of((chunk * mm_tiles + t) * LANES, LANES), LANES)
                inverse = inverses[rows, where]
                cube = inverse * inverse * inverse
                inverses[rows, where] = cube
                pull = cube * mq
                fx = fx + pull * (px - mx)
                fy = fy + pull * (py - my)
                fz = fz + pull * (pz - mz)
            acc_x[rows, :], acc_y[rows, :], acc_z[rows, :] = fx, fy, fz
            return inner

        return lax.fori_loop(0, nz * atoms // FORCE_ROWS, group, carry)

    early = min(EARLY, nq)
    lax.fori_loop(0, early, pull_chunk, 0)
    wait_all(POT_X, row_x, pot_x)
    pot_z[ring] = total(pot_x, nx)
    send_all(POT_Z, far, lambda p: pot_z.at[ring], pot_z)
    late = max(early, nq - LATE)
    lax.fori_loop(early, late, pull_chunk, 0)

    wait_all(POT_Z, far, pot_z)
    pot_q[q] = total(pot_z, rings) * coupling
    send_all(POT_Q, plane, lambda p: pot_q.at[q], pot_q)
    lax.fori_loop(late, nq, pull_chunk, 0)

    def gather_force(p, carry):
        qmf_mine[p, 0:1, :] = lines(acc_x, p)
        qmf_mine[p, 1:2, :] = lines(acc_y, p)
        qmf_mine[p, 2:3, :] = lines(acc_z, p)
        return carry

    lax.fori_loop(0, nz, gather_force, 0)
    qmf_z[ring] = qmf_mine[z]
    send_all(QMF_Z, far, lambda p: qmf_mine.at[p % nz], qmf_z)

    wait_all(CODE_Q, plane, code_q)
    codes = jnp.concatenate([code_q[p] for p in range(nq)], axis=0).astype(BF16)
    gain = gain_ref[...]
    table = table_wide[...].astype(BF16)
    bases, lives = [], []
    for k in range(neighbours + 1):
        rows = slice(k * atoms, (k + 1) * atoms)
        picked = jnp.dot(owner_hot[rows, 0:blocks], codes, preferred_element_type=F32)
        code = jnp.sum(picked * slot_hot[rows, :], axis=1, keepdims=True)
        lives.append((code >= 0).astype(F32))
        kinds = (lane.astype(F32) == code).astype(F32).astype(BF16)
        bases.append(jnp.dot(kinds, table, preferred_element_type=F32))
    wait_all(POT_Q, plane, pot_q)
    pieces = split3(jnp.concatenate([pot_q[p] for p in range(nq)], axis=0))
    neighbour = jnp.zeros((atoms, LANES), F32)
    for k in range(neighbours + 1):
        rows = slice(k * atoms, (k + 1) * atoms)
        hot = owner_hot[rows, 0:blocks]
        slots = slot_hot[rows, :]
        picked = [jnp.dot(hot, piece, preferred_element_type=F32) for piece in pieces]
        potential = jnp.sum((picked[0] + picked[1] + picked[2]) * slots, axis=1, keepdims=True)
        live = lives[k]
        start = (live * (bases[k] + potential * gain)).astype(BF16)
        if k < neighbours:
            neighbour = neighbour + start.astype(F32)
    mixed = start.astype(F32) + jnp.dot(
        neighbour.astype(BF16), message_ref[...], preferred_element_type=F32
    )
    before = jnp.dot(mixed.astype(BF16), hidden_ref[...], preferred_element_type=F32)
    sigma = jax.nn.sigmoid(before)
    active = before * sigma
    charge_part = live * jnp.sum(active * readout_ref[...], axis=1, keepdims=True)
    back_active = live * (energy_ref[...] + potential * readout_ref[...])
    back_before = (back_active * sigma * (1.0 + before * (1.0 - sigma))).astype(BF16)
    nt = (((1,), (1,)), ((), ()))
    back_mixed = lax.dot_general(back_before, hidden_ref[...], nt, preferred_element_type=F32)
    back_sum = lax.dot_general(
        back_mixed.astype(BF16), message_ref[...], nt, preferred_element_type=F32
    ).astype(BF16)
    out_going = jnp.sum(back_sum.astype(F32) * gain, axis=1, keepdims=True)
    staying = jnp.sum(back_mixed * gain, axis=1, keepdims=True) + charge_part
    spread = jnp.zeros((blocks, LANES), F32)
    parts_out, parts_stay = split3(out_going), split3(staying)
    for k in range(neighbours + 1):
        rows = slice(k * atoms, (k + 1) * atoms)
        slots = slot_hot[rows, :]
        for part in parts_out if k < neighbours else parts_stay:
            spread = spread + jnp.dot(
                owner_hot_t[0:blocks, rows],
                (slots * part.astype(F32)).astype(BF16),
                preferred_element_type=F32,
            )
    for p in range(nq):
        grad_mine[p] = spread[p * nz : (p + 1) * nz, :]
    send_all(GRAD_Q, plane, lambda p: grad_mine.at[p], grad_q)
    grad_q[q] = grad_mine[q]
    energy_part = live * jnp.sum(active * energy_ref[...], axis=1, keepdims=True)
    atom_energy = energy_part + charge_part * potential
    atom_energy_ref[...] = jnp.sum(
        jnp.where(lane == row, atom_energy, 0.0), axis=0, keepdims=True
    )

    def split_rows(g, carry):
        rows = pl.ds(pl.multiple_of(g * FORCE_ROWS, FORCE_ROWS), FORCE_ROWS)
        cube = inverses[rows, :]
        high = cube.astype(BF16)
        cube_high[rows, :] = high
        cube_low[rows, :] = (cube - high.astype(F32)).astype(BF16)
        return carry

    lax.fori_loop(0, nz * atoms // FORCE_ROWS, split_rows, 0)
    wait_all(GRAD_Q, plane, grad_q)
    grad_n[z] = total(grad_q, nq)
    send_all(GRAD_N, near, lambda p: grad_n.at[z], grad_n)
    wait_all(QMF_Z, far, qmf_z)
    qmf_x[x] = total(qmf_z, rings)
    send_all(QMF_X, row_x, lambda p: qmf_x.at[x], qmf_x)
    wait_all(GRAD_N, near, grad_n)
    live_plane = (code_q[q] >= 0).astype(F32)
    grad_sum[...] = live_plane * total(grad_n, nz)

    effective = jnp.concatenate([grad_sum[p : p + 1, :] for p in range(nz)], axis=1)
    weights = qm_lines[...] * effective
    high = weights.astype(BF16).astype(F32)
    weights = jnp.concatenate([high, weights - high], axis=0).astype(BF16)

    def push_pair(y):
        width = 2 * mm_tiles * LANES
        where = pl.ds(pl.multiple_of(y * width, width), width)
        sums = jnp.dot(weights, cube_high[:, where], preferred_element_type=F32)
        sums = sums + jnp.dot(weights, cube_low[:, where], preferred_element_type=F32)
        sums = sums[0:8, :] + sums[8:16, :]
        for c in range(2):
            part = sums[:, c * width // 2 : (c + 1) * width // 2]
            mmf_mine[2 * y + c] = part[1:4, :] - part[0:1, :] * mm_all[2 * y + c, 0:3, :]

    rows_y = nq // 2

    def push_step(k, carry):
        step = rows_y // 2 + zigzag(k)
        push_pair((q // 2 + step) % rows_y)
        for c in range(2):
            outgoing(MMF_Q, plane, lambda p: mmf_mine.at[p], mmf_q, 2 * step + c).start()
        return carry

    lax.fori_loop(1, rows_y, push_step, 0)
    push_pair(q // 2)
    outgoing(MMF_Q, plane, lambda p: mmf_mine.at[p], mmf_q, 1).start()
    mmf_q[q] = mmf_mine[q]
    sent_all(QM_N, near, lambda p: qm_all.at[z], qm_all)
    sent_all(MM_Q, plane, lambda p: mm_all.at[q], mm_all)
    sent_all(POT_X, row_x, lambda p: pot_x.at[x], pot_x)
    sent_all(POT_Z, far, lambda p: pot_z.at[ring], pot_z)
    sent_all(POT_Q, plane, lambda p: pot_q.at[q], pot_q)
    sent_all(CODE_Q, plane, lambda p: code_q.at[q], code_q)
    sent_all(QMF_Z, far, lambda p: qmf_mine.at[p % nz], qmf_z)
    sent_all(GRAD_Q, plane, lambda p: grad_mine.at[p], grad_q)
    sent_all(GRAD_N, near, lambda p: grad_n.at[z], grad_n)
    wait_all(QMF_X, row_x, qmf_x)
    qm_force_ref[...] = total(qmf_x, nx) * (grad_sum[pl.ds(z, 1), :] * coupling)
    sent_all(QMF_X, row_x, lambda p: qmf_x.at[x], qmf_x)
    sent_all(MMF_Q, plane, lambda p: mmf_mine.at[p], mmf_q)
    wait_all(MMF_Q, plane, mmf_q)
    mm_force_ref[...] = total(mmf_q, nq) * (charge_ref[...] * -coupling)


def on_device(
    nz,
    nq,
    nr,
    qm_pos,
    species,
    qm_count,
    ghost_owner,
    ghost_slot,
    mm_pos,
    mm_charge,
    species_table,
    potential_gain,
    message_weight,
    hidden_weight,
    energy_readout,
    charge_readout,
):
    atoms = qm_pos.shape[1]
    mm_here = mm_pos.shape[1]
    nx = nr // 2
    coupling = float(mm_here * nz * nq * nr) ** (-0.5)
    here = nz * atoms
    groups = ghost_owner.shape[1] + 1
    hot_rows = -(-nz * nq // 16) * 16
    arguments = (
        qm_pos,
        species[None, :],
        qm_count[None, :],
        ghost_owner.T,
        ghost_slot.T,
        mm_pos,
        mm_charge[None, :],
        species_table,
        potential_gain[None, :],
        message_weight,
        hidden_weight,
        energy_readout[None, :],
        charge_readout[None, :],
    )
    small = lambda *shape: pltpu.VMEM(shape, F32)
    vmem = pl.BlockSpec(memory_space=pltpu.VMEM)
    hbm = pl.BlockSpec(memory_space=pltpu.HBM)
    atom_energy, qm_force, mm_force = pl.pallas_call(
        functools.partial(kernel, nz, nq, nx, coupling),
        out_shape=(
            jax.ShapeDtypeStruct((1, atoms), F32),
            jax.ShapeDtypeStruct((3, atoms), F32),
            jax.ShapeDtypeStruct((3, mm_here), F32),
        ),
        in_specs=[hbm] * 7 + [vmem] + [hbm] * 5,
        out_specs=(vmem,) * 3,
        scratch_shapes=[
            small(nq, 4, mm_here),
            small(nz, 4, atoms),
            small(nx, nz, atoms),
            small(2 * nz, nz, atoms),
            small(nq, nz, atoms),
            small(nq, nz, atoms),
            small(nq, nz, atoms),
            small(nq, nz, atoms),
            small(nz, nz, atoms),
            small(nz, atoms),
            small(nz, 3, atoms),
            small(2 * nz, 3, atoms),
            small(nx, 3, atoms),
            small(nq, 3, mm_here),
            small(nq, 3, mm_here),
            *[small(here, LANES)] * 6,
            small(here, nq * mm_here),
            pltpu.VMEM((here, nq * mm_here), BF16),
            pltpu.VMEM((here, nq * mm_here), BF16),
            pltpu.VMEM((48, nq * mm_here), BF16),
            small(1, nq * mm_here),
            small(8, here),
            small(LANES, LANES),
            pltpu.VMEM((groups * atoms, LANES), BF16),
            pltpu.VMEM((hot_rows, groups * atoms), BF16),
            small(groups * atoms, LANES),
            *[pltpu.VMEM(a.shape, a.dtype) for k, a in enumerate(arguments) if k != TABLE],
            pltpu.SemaphoreType.DMA((12,)),
            pltpu.SemaphoreType.DMA((11, max(2 * nz, nq, nx))),
            pltpu.SemaphoreType.DMA((11, max(2 * nz, nq, nx))),
        ],
        compiler_params=pltpu.CompilerParams(
            collective_id=0, has_side_effects=True, vmem_limit_bytes=55176 * 2**10
        ),
    )(*arguments)
    return (atom_energy[0], qm_force, mm_force)


def solution(mesh):
    blocks, nr = mesh.shape["blk"], mesh.shape["rep"]
    nq = min(8, blocks // 2)
    placed = (
        P(None, "blk"),
        P("blk"),
        P("blk"),
        P("blk", None),
        P("blk", None),
        P(None, ("blk", "rep")),
        P(("blk", "rep")),
        P(),
        P(),
        P(),
        P(),
        P(),
        P(),
    )
    return jax.shard_map(
        functools.partial(on_device, blocks // nq, nq, nr),
        mesh=mesh,
        in_specs=placed,
        out_specs=(P("blk"), P(None, "blk"), P(None, ("blk", "rep"))),
        check_vma=False,
    )
```
